32 devices in a mesh: ctx: 8 (over z, y), head: 4 (over x, core).
Axes of the slice: x: 2, y: 2, z: 4, core: 2. Of those that a mesh axis runs over, the one named last changes fastest.
Arguments:
- queries: bfloat16 [1024, 4096], P('ctx', 'head'), may hold values from -12 to 12
- keys: bfloat16 [1024, 512], P('ctx', 'head'), may hold values from -6 to 6
- values: bfloat16 [1024, 512], P('ctx', 'head'), may hold values from -18 to 18
- doc_ids: int32 [1024], P('ctx'), may hold values from 0 to 15, never falling along the last dimension, each value on 1 to 768 neighbouring positions
- plan: int32 [8, 8], P('ctx'), may hold values from 0 to 7, each once within a row
- w_out: bfloat16 [4096, 8192], P('head', 'ctx'), may hold values from -0.09375 to 0.09375
Outputs:
- output: bfloat16 [1024, 8192], P('ctx', 'head')
The draws below stay inside these ranges and needn't reach their ends.
Inputs may be any that keep to these rules, and one draw needn't show every extreme that they name: doc_ids never fall along the window; every one of the 16 documents holds 1 to 768 positions, and one holds exactly 768. Each row of plan is a permutation of the device indices along ctx.
All inputs are finite; a program needn't handle non-finite values.
Results may differ from the reference program's by a relative error of at most 0.01.
Values may be sent and summed in bfloat16 or wider, within the bound.
No kernel may reach another device: no remote copies, remote signals or barrier semaphores. Data moves between devices by JAX's collectives and lax.ppermute only.
A program may use at most 64 MiB of HBM per device.

```python
import math
import jax
import jax.numpy as jnp
import numpy as np
from jax import lax

TOK_DEV = 128
HEADS = 32
KV_HEADS = 4
HEAD_DIM = 128
D = 8192
DOCS = 16
TOKENS = 1024
PIECE = 16
MAXDOC = 768
N_CTX = 8
N_HEAD = 4


def draw_queries(key, part):
    main_key = jax.random.fold_in(key, 1)
    result = jnp.clip(2.0 * jax.random.normal(main_key, (TOKENS, HEADS * HEAD_DIM), jnp.float32), -12.0, 12.0)
    return result.astype(jnp.bfloat16)


def draw_keys(key, part):
    main_key = jax.random.fold_in(key, 2)
    result = jnp.clip(jax.random.normal(main_key, (TOKENS, KV_HEADS * HEAD_DIM), jnp.float32), -6.0, 6.0)
    return result.astype(jnp.bfloat16)


def level_of(stream_key, dims, shards, low, largest):
    factor_of = 1.0
    for position, shards_of in shards:
        draws = jax.random.uniform(jax.random.fold_in(jax.random.fold_in(stream_key, 6), position), (shards_of,), jnp.float32, low / len(shards), largest / len(shards))
        factor_of = factor_of * jnp.repeat(jnp.exp(draws), dims[position] // shards_of).reshape((-1,) + (1,) * (len(dims) - 1 - position))
    return factor_of


def length_profile(number_of, total, most, skew):
    portions = [(1 << 20) // math.isqrt(standing ** skew) + 1 for standing in range(2, number_of + 1)]
    surplus, counts = total - most - (number_of - 1), [1] * (number_of - 1)
    while surplus > 0:
        free = [i for i in range(number_of - 1) if counts[i] < most]
        whole, left = sum([portions[i] for i in free]), surplus
        for i in free:
            more = min(most - counts[i], max(1, left * portions[i] // whole), surplus)
            counts[i] = counts[i] + more
            surplus = surplus - more
    return np.array([most] + counts)


def uneven(stream_key, number_of, total, reach, slope):
    if number_of == 2:
        one = jax.random.randint(stream_key, (), max(1, total - reach), min(reach, total - 1) + 1)
        return jnp.stack([one, total - one])
    lengths = jnp.asarray(length_profile(number_of, total, reach, slope), jnp.int32)
    twos = (number_of - 1) // 2
    giver, sink = lengths[1:1 + 2 * twos:2], lengths[2:2 + 2 * twos:2]
    margin = jnp.minimum(giver - 1, reach - sink)
    moved = jax.random.randint(jax.random.fold_in(stream_key, 1), (twos,), 0, 1 << 20) % (margin + 1)
    lengths = lengths.at[1:1 + 2 * twos:2].set(giver - moved).at[2:2 + 2 * twos:2].set(sink + moved)
    return lengths[jax.random.permutation(jax.random.fold_in(stream_key, 2), number_of)]


def gaussian(rng, dims, scale, bound, cuts=(), kind=jnp.bfloat16):
    drawn = scale * jax.random.normal(rng, dims, jnp.float32)
    if cuts:
        drawn = drawn * level_of(rng, dims, cuts, -0.22, 0.18)
    return jnp.clip(drawn, -bound, bound).astype(kind)


def setup_inputs(seed: int = 0) -> dict:
    key_of = jax.random.split(jax.random.key(seed), 7)
    return {
        "queries": draw_queries(jax.random.fold_in(key_of[6], 71), 0),
        "keys": draw_keys(jax.random.fold_in(key_of[6], 71), 0),
        "values": gaussian(key_of[2], (TOKENS, KV_HEADS * HEAD_DIM), 3.0, 18.0, ((0, 8), (1, 4))),
        "doc_ids": jnp.searchsorted(jnp.cumsum(uneven(key_of[3], DOCS, TOKENS, MAXDOC, 2)), jnp.arange(TOKENS), side="right").astype(jnp.int32),
        "plan": jax.vmap(lambda own: jax.random.permutation(own, N_CTX))(jax.random.split(key_of[4], N_CTX)).reshape((N_CTX, N_CTX)).astype(jnp.int32),
        "w_out": gaussian(key_of[5], (HEADS * HEAD_DIM, D), (HEADS * HEAD_DIM) ** -0.5, 0.09375, ((0, 4), (1, 8))),
    }


NEG_FILL = -1e+30

def head_attention(operands, allowed, score_scale):
    query_head, key_head, value_head = operands
    scores = jnp.einsum('bgd,ld->gbl', query_head.astype(jnp.float32), key_head.astype(jnp.float32)) * score_scale
    scores = jnp.where(allowed[None], scores, NEG_FILL)
    row_max = lax.optimization_barrier(jnp.max(scores, axis=-1, keepdims=True))
    expo = jnp.where(allowed[None], jnp.exp(scores - row_max), 0.0)
    totals = lax.optimization_barrier(jnp.sum(expo, axis=-1))
    rounded = lax.optimization_barrier(expo.astype(jnp.bfloat16)).astype(jnp.float32)
    numer = jnp.einsum('gbl,ld->gbd', rounded, value_head.astype(jnp.float32))
    return numer / totals[..., None]

def reference(queries, keys, values, doc_ids, plan, w_out):
    doc_range = jnp.arange(DOCS, dtype=jnp.int32)
    doc_first = lax.optimization_barrier(jnp.sum((doc_ids[None, :] < doc_range[:, None]).astype(jnp.int32), axis=1))
    doc_start = doc_first[doc_ids]
    group_size = HEADS // KV_HEADS
    score_scale = 1.0 / math.sqrt(HEAD_DIM)
    q_all = queries.reshape(TOKENS, KV_HEADS, group_size, HEAD_DIM).transpose(1, 0, 2, 3)
    k_all = keys.reshape(TOKENS, KV_HEADS, HEAD_DIM).transpose(1, 0, 2)
    v_all = values.reshape(TOKENS, KV_HEADS, HEAD_DIM).transpose(1, 0, 2)
    block_size = min(512, TOKENS)
    results = []
    for block_index in range(TOKENS // block_size):
        lower = block_index * block_size
        upper = lower + block_size
        row_pos = jnp.arange(lower, upper, dtype=jnp.int32)
        row_start = doc_start[lower:upper]
        key_pos = jnp.arange(upper, dtype=jnp.int32)
        allowed = (key_pos[None, :] >= row_start[:, None]) & (key_pos[None, :] <= row_pos[:, None])
        per_head = lax.map(partial_head(allowed, score_scale), (q_all[:, lower:upper], k_all[:, :upper], v_all[:, :upper]))
        block_out = per_head.transpose(2, 0, 1, 3).reshape(block_size, HEADS * HEAD_DIM)
        results.append(block_out.astype(jnp.bfloat16))
    attended = jnp.concatenate(results, axis=0)
    slot_index = jnp.arange(N_CTX, dtype=jnp.int32)
    within = jnp.arange(PIECE, dtype=jnp.int32)
    source_pos = slot_index[None, :, None] * TOK_DEV + plan.T[:, :, None] * PIECE + within[None, None, :]
    arranged = attended[source_pos.reshape(-1).astype(jnp.int32)]
    rows_per = HEADS * HEAD_DIM // N_HEAD
    summed = jnp.zeros((TOKENS, D), jnp.float32)
    for group_index in range(N_HEAD):
        lower = group_index * rows_per
        upper = lower + rows_per
        partial_sum = jnp.dot(arranged[:, lower:upper], w_out[lower:upper], preferred_element_type=jnp.float32)
        summed = summed + lax.optimization_barrier(partial_sum.astype(jnp.bfloat16)).astype(jnp.float32)
    return summed.astype(jnp.bfloat16)

def partial_head(allowed, score_scale):

    def run_head(operands):
        return head_attention(operands, allowed, score_scale)
    return run_head
```

```python
import functools
import math

import jax
import jax.numpy as jnp
from jax import lax
from jax.experimental import pallas as pl
from jax.experimental.pallas import tpu as pltpu
from jax.sharding import PartitionSpec as P

HEAD_DIM = 128
DOCS = 16
META = 16
NEG_FILL = -1e30
VMEM_LIMIT = 56 * 1024 * 1024

ANY = pl.BlockSpec(memory_space=pl.ANY)
VMEM = pl.BlockSpec(memory_space=pltpu.VMEM)
SMEM = pl.BlockSpec(memory_space=pltpu.SMEM)


def pack_kernel(parts, heads, plan_ref, q_ref, k_ref, v_ref, ids_ref, out_ref):
    rows = q_ref.shape[0]
    piece = rows // parts
    lane = lax.broadcasted_iota(jnp.int32, (1, rows), 1)
    source = jnp.zeros((1, rows), jnp.int32)
    for j in range(parts):
        p = plan_ref[0, j]
        for h in range(heads):
            out_ref[h * rows + j * piece : h * rows + (j + 1) * piece, :] = q_ref[
                pl.ds(pl.multiple_of(p * piece, piece), piece),
                h * HEAD_DIM : (h + 1) * HEAD_DIM,
            ]
        source = jnp.where(
            (lane >= j * piece) & (lane < (j + 1) * piece), (p - j) * piece + lane, source
        )
    base = heads * rows
    out_ref[base : base + rows, :] = k_ref[...]
    out_ref[base + rows : base + 2 * rows, :] = v_ref[...]
    ids = ids_ref[...].astype(jnp.float32)
    row = lax.broadcasted_iota(jnp.int32, (META, rows), 0)
    from_row = lax.broadcasted_iota(jnp.int32, (rows, rows), 0)
    chosen = (from_row == source).astype(jnp.float32)
    ids_rows = jnp.broadcast_to(ids, (META, rows))
    ids_moved = jnp.dot(ids_rows, chosen, preferred_element_type=jnp.float32)
    meta = jnp.where(
        row == 0,
        ids_rows,
        jnp.where(row == 1, ids_moved, jnp.broadcast_to(source.astype(jnp.float32), (META, rows))),
    )
    out_ref[base + 2 * rows :, :] = meta.astype(jnp.bfloat16)


def attend_project_kernel(parts, heads, scale, w_ref, *refs):
    blocks, (send_ref, keep_ref, held, rows_ref, w_held, sems) = refs[:parts], refs[parts:]
    rows = send_ref.shape[0] * 2 // parts
    piece = rows // parts
    base = heads * rows
    me = lax.axis_index("ctx")
    other = 1 - lax.rem(lax.axis_index("head"), 2)
    copies = [
        pltpu.make_async_copy(blocks[k], held.at[jnp.bitwise_xor(me, k)], sems.at[k])
        for k in range(parts)
    ]
    w_copy = pltpu.make_async_copy(w_ref, w_held, sems.at[parts])
    for copy in copies:
        copy.start()
    w_copy.start()
    for copy in copies:
        copy.wait()
    for d in range(parts):
        span = (d + 1) * rows
        meta = held[d, base + 2 * rows :, :].astype(jnp.float32)
        turned = meta.T
        q_ids, q_pos = turned[:, 1:2], turned[:, 2:3]
        k_ids = jnp.concatenate(
            [held[b, base + 2 * rows :, :].astype(jnp.float32)[0:1] for b in range(d + 1)], axis=1
        )
        k_pos = lax.broadcasted_iota(jnp.int32, (1, span), 1) - d * rows
        allowed = (k_ids == q_ids) & (k_pos.astype(jnp.float32) <= q_pos)
        bias = jnp.where(allowed, 0.0, NEG_FILL)

        def one_head(h, carry, d=d, span=span, bias=bias):
            q = held[d, pl.ds(pl.multiple_of(h * rows, rows), rows), :]
            keys = held[: d + 1, base : base + rows, :].reshape(span, HEAD_DIM)
            vals = held[: d + 1, base + rows : base + 2 * rows, :].reshape(span, HEAD_DIM)
            s = lax.dot_general(q, keys, (((1,), (1,)), ((), ())), preferred_element_type=jnp.float32)
            s = s + bias
            top = jnp.max(s, axis=1, keepdims=True)
            e = jnp.exp2((s - top) * (scale * math.log2(math.e)))
            total = jnp.sum(e, axis=1, keepdims=True)
            o = jnp.dot(e.astype(jnp.bfloat16), vals, preferred_element_type=jnp.float32) / total
            o = o.astype(jnp.bfloat16)
            for j in range(parts):
                at = (j // 2) * rows + d * piece
                rows_ref[
                    j % 2, at : at + piece, pl.ds(pl.multiple_of(h * HEAD_DIM, HEAD_DIM), HEAD_DIM)
                ] = o[j * piece : (j + 1) * piece, :]
            return carry

        lax.fori_loop(0, heads, one_head, 0)
    w_copy.wait()
    send_ref[...] = jnp.dot(
        rows_ref[other], w_held[...], preferred_element_type=jnp.float32
    ).astype(jnp.bfloat16)
    keep_ref[...] = jnp.dot(
        rows_ref[1 - other], w_held[...], preferred_element_type=jnp.float32
    ).astype(jnp.bfloat16)


def pair_sum_kernel(group, half, keep_ref, got_ref, *out_refs):
    count = len(out_refs)
    rows = keep_ref.shape[0] // count
    mine = lax.rem(lax.axis_index("ctx"), group) * half + lax.axis_index("head") // 2
    for k, out_ref in enumerate(out_refs):
        at = pl.ds(pl.multiple_of(jnp.bitwise_xor(mine, k) * rows, rows), rows)
        out_ref[...] = (keep_ref[at, :].astype(jnp.float32) + got_ref[at, :].astype(jnp.float32)).astype(
            jnp.bfloat16
        )


def final_kernel(group, half, *refs):
    blocks, out_ref = refs[:-1], refs[-1]
    cols = blocks[0].shape[1]
    high = lax.axis_index("ctx") // 2
    for first in range(0, len(blocks), half):
        part = lax.div(jnp.bitwise_xor(high, first), half)
        total = blocks[first][...].astype(jnp.float32)
        for k in range(first + 1, first + half):
            total = total + blocks[k][...].astype(jnp.float32)
        out_ref[:, pl.ds(pl.multiple_of(part * cols, cols), cols)] = total.astype(jnp.bfloat16)


def spread_over_ctx(block, parts):
    def moved(x, k):
        return lax.ppermute(x, "ctx", [(i, i ^ k) for i in range(parts)])

    got = {0: block}
    for k in range(2, parts, 2):
        got[k] = moved(block, k)
    got[1] = moved(block, 1)
    for k in range(2, parts, 2):
        got[k + 1] = moved(got[k], 1)
    return [got[k] for k in range(parts)]


def packed_body(groups, queries, keys, values, doc_ids, plan, w_out):
    parts = lax.axis_size("ctx")
    rows = queries.shape[0]
    heads = queries.shape[1] // HEAD_DIM
    width = w_out.shape[1]
    group, half = parts // groups, groups // 2
    bf16 = jnp.bfloat16
    params = pltpu.CompilerParams(vmem_limit_bytes=VMEM_LIMIT)
    block_rows = (heads + 2) * rows + META
    block = pl.pallas_call(
        functools.partial(pack_kernel, parts, heads),
        out_shape=jax.ShapeDtypeStruct((block_rows, HEAD_DIM), bf16),
        in_specs=[SMEM, VMEM, VMEM, VMEM, VMEM],
        out_specs=VMEM,
        compiler_params=params,
        name="pack",
    )(plan, queries, keys, values, doc_ids.reshape(1, rows))
    blocks = spread_over_ctx(block, parts)
    tokens = parts * rows
    send, keep = pl.pallas_call(
        functools.partial(attend_project_kernel, parts, heads, 1.0 / math.sqrt(HEAD_DIM)),
        out_shape=[jax.ShapeDtypeStruct((tokens // 2, width), bf16)] * 2,
        in_specs=[ANY] * (1 + parts),
        out_specs=[VMEM, VMEM],
        scratch_shapes=[
            pltpu.VMEM((parts, block_rows, HEAD_DIM), bf16),
            pltpu.VMEM((2, tokens // 2, heads * HEAD_DIM), bf16),
            pltpu.VMEM(w_out.shape, bf16),
            pltpu.SemaphoreType.DMA((parts + 1,)),
        ],
        compiler_params=params,
        name="attend_project",
    )(w_out, *blocks)
    got = lax.ppermute(send, "head", [(g, g ^ 1) for g in range(groups)])
    count = parts // 2
    sums = pl.pallas_call(
        functools.partial(pair_sum_kernel, group, half),
        out_shape=[jax.ShapeDtypeStruct((rows, width), bf16)] * count,
        in_specs=[VMEM, VMEM],
        out_specs=[VMEM] * count,
        compiler_params=params,
        name="pair_sum",
    )(keep, got)
    arrived = []
    for k in range(count):
        pairs = []
        for c in range(parts):
            for g in range(groups):
                high = ((c % group) * half + g // 2) ^ k
                pairs.append((c * groups + g, (high * 2 + g % 2) * groups + c // group))
        arrived.append(lax.ppermute(sums[k], ("ctx", "head"), pairs))
    return pl.pallas_call(
        functools.partial(final_kernel, group, half),
        out_shape=jax.ShapeDtypeStruct((rows, group * width), bf16),
        in_specs=[VMEM] * count,
        out_specs=VMEM,
        compiler_params=params,
        name="final_sum",
    )(*arrived)


def spread_rows(block, order, parts):
    shaped = block.reshape(parts, block.shape[0] // parts, block.shape[1])
    return jnp.take(shaped, order, axis=0).reshape(block.shape)


def attend(query_rows, row_pos, row_start, all_keys, all_values):
    n_rows = query_rows.shape[0]
    kv_local = all_keys.shape[1] // HEAD_DIM
    group_size = query_rows.shape[1] // all_keys.shape[1]
    q_heads = query_rows.reshape(n_rows, kv_local, group_size, HEAD_DIM).transpose(1, 0, 2, 3)
    q_heads = q_heads.reshape(kv_local, n_rows * group_size, HEAD_DIM)
    pos_rows = jnp.repeat(row_pos, group_size)
    start_rows = jnp.repeat(row_start, group_size)
    q_block = min(n_rows, max(1, 512 // group_size))
    block_rows = q_block * group_size
    n_qblocks = n_rows // q_block
    score_scale = 1.0 / math.sqrt(HEAD_DIM)
    total_keys = all_keys.shape[0]
    key_size = math.gcd(total_keys, 512)
    n_kblocks = total_keys // key_size
    key_tiles = all_keys.reshape(n_kblocks, key_size, kv_local, HEAD_DIM)
    value_tiles = all_values.reshape(n_kblocks, key_size, kv_local, HEAD_DIM)
    initial = (
        jnp.full((kv_local, n_rows * group_size), NEG_FILL, jnp.float32),
        jnp.zeros((kv_local, n_rows * group_size), jnp.float32),
        jnp.zeros((kv_local, n_rows * group_size, HEAD_DIM), jnp.float32),
    )

    def one_query_block(block_index, state):
        run_max, run_sum, run_acc = state
        offset = block_index * block_rows
        q_part = lax.dynamic_slice_in_dim(q_heads, offset, block_rows, 1)
        pos_part = lax.dynamic_slice_in_dim(pos_rows, offset, block_rows, 0)
        start_part = lax.dynamic_slice_in_dim(start_rows, offset, block_rows, 0)
        first_block = jnp.clip(jnp.min(start_part) // key_size, 0, n_kblocks)
        last_block = jnp.clip(jnp.max(pos_part) // key_size + 1, 0, n_kblocks)

        def add_tile(key_index, inner):
            block_max, block_sum, block_acc = inner
            key_tile = lax.dynamic_index_in_dim(key_tiles, key_index, 0, keepdims=False)
            value_tile = lax.dynamic_index_in_dim(value_tiles, key_index, 0, keepdims=False)
            scores = (
                jnp.einsum("grd,kgd->grk", q_part, key_tile, preferred_element_type=jnp.float32)
                * score_scale
            )
            key_pos = key_index * key_size + jnp.arange(key_size, dtype=jnp.int32)
            allowed = (key_pos[None, :] >= start_part[:, None]) & (
                key_pos[None, :] <= pos_part[:, None]
            )
            scores = jnp.where(allowed[None], scores, NEG_FILL)
            new_max = jnp.maximum(block_max, jnp.max(scores, axis=-1))
            expo = jnp.where(allowed[None], jnp.exp(scores - new_max[..., None]), 0.0)
            rescale = jnp.exp(block_max - new_max)
            block_sum = block_sum * rescale + jnp.sum(expo, axis=-1)
            block_acc = block_acc * rescale[..., None] + jnp.einsum(
                "grk,kgd->grd",
                expo.astype(jnp.bfloat16),
                value_tile,
                preferred_element_type=jnp.float32,
            )
            return (new_max, block_sum, block_acc)

        def one_key_block(key_index, inner):
            tile_low = key_index * key_size
            tile_high = tile_low + key_size - 1
            meets = jnp.any((start_part <= tile_high) & (pos_part >= tile_low))
            return lax.cond(
                meets, lambda carried: add_tile(key_index, carried), lambda carried: carried, inner
            )

        inner = (
            lax.dynamic_slice_in_dim(run_max, offset, block_rows, 1),
            lax.dynamic_slice_in_dim(run_sum, offset, block_rows, 1),
            lax.dynamic_slice_in_dim(run_acc, offset, block_rows, 1),
        )
        new_max, new_sum, new_acc = lax.fori_loop(first_block, last_block, one_key_block, inner)
        run_max = lax.dynamic_update_slice_in_dim(run_max, new_max, offset, 1)
        run_sum = lax.dynamic_update_slice_in_dim(run_sum, new_sum, offset, 1)
        run_acc = lax.dynamic_update_slice_in_dim(run_acc, new_acc, offset, 1)
        return (run_max, run_sum, run_acc)

    final_max, final_sum, final_acc = lax.fori_loop(0, n_qblocks, one_query_block, initial)
    result = final_acc / final_sum[..., None]
    result = result.reshape(kv_local, n_rows, group_size, HEAD_DIM).transpose(1, 0, 2, 3)
    return result.reshape(n_rows, kv_local * group_size * HEAD_DIM).astype(jnp.bfloat16)


def body(queries, keys, values, doc_ids, plan, w_out):
    n_rows = queries.shape[0]
    parts = lax.axis_size("ctx")
    my_index = lax.axis_index("ctx")
    all_ids, all_plan = (
        lax.all_gather(doc_ids, "ctx", axis=0, tiled=True),
        lax.all_gather(plan, "ctx", axis=0, tiled=True),
    )
    all_keys, all_values = (
        lax.all_gather(keys, "ctx", axis=0, tiled=True),
        lax.all_gather(values, "ctx", axis=0, tiled=True),
    )
    doc_range = jnp.arange(DOCS, dtype=jnp.int32)
    doc_first = jnp.sum((all_ids[None, :] < doc_range[:, None]).astype(jnp.int32), axis=1)
    local_pos = my_index * n_rows + jnp.arange(n_rows, dtype=jnp.int32)
    ids_here = jnp.take(all_ids, local_pos)
    local_out = attend(
        queries,
        local_pos,
        jnp.sum(jnp.where(ids_here[:, None] == doc_range[None, :], doc_first[None, :], 0), axis=1),
        all_keys,
        all_values,
    )
    attended = lax.all_to_all(
        spread_rows(local_out, plan[0], parts), "ctx", split_axis=0, concat_axis=0, tiled=True
    )
    stacked = jnp.dot(
        lax.all_gather(attended, "ctx", axis=0, tiled=True),
        w_out,
        preferred_element_type=jnp.float32,
    )
    partial_sum = lax.all_to_all(
        stacked.astype(jnp.bfloat16), "ctx", split_axis=0, concat_axis=1, tiled=True
    ).astype(stacked.dtype)
    summed = lax.psum_scatter(
        partial_sum.astype(jnp.bfloat16), "head", scatter_dimension=1, tiled=True
    )
    return summed


def fits(parts, groups, rows, width):
    powers = all(n & (n - 1) == 0 for n in (parts, groups))
    window = parts * rows * width * 2
    whole = rows % (16 * parts) == 0 and groups % 2 == 0 and parts % groups == 0
    return powers and whole and 8 * window <= VMEM_LIMIT


def solution(mesh):
    parts, groups = mesh.shape["ctx"], mesh.shape["head"]

    def one_device(queries, keys, values, doc_ids, plan, w_out):
        one_pair = keys.shape[1] == HEAD_DIM
        if one_pair and fits(parts, groups, queries.shape[0], queries.shape[1]):
            return packed_body(groups, queries, keys, values, doc_ids, plan, w_out)
        return body(queries, keys, values, doc_ids, plan, w_out)

    return jax.shard_map(
        one_device,
        mesh=mesh,
        in_specs=(
            P("ctx", "head"),
            P("ctx", "head"),
            P("ctx", "head"),
            P("ctx"),
            P("ctx", None),
            P("head", "ctx"),
        ),
        out_specs=P("ctx", "head"),
        check_vma=False,
    )
```

```python
import functools
import math

import jax
import jax.numpy as jnp
from jax import lax
from jax.experimental import pallas as pl
from jax.experimental.pallas import tpu as pltpu
from jax.sharding import PartitionSpec as P

HEAD_DIM = 128
DOCS = 16
META = 16
NEG_FILL = -1e30
VMEM_LIMIT = 56 * 1024 * 1024

ANY = pl.BlockSpec(memory_space=pl.ANY)
VMEM = pl.BlockSpec(memory_space=pltpu.VMEM)
SMEM = pl.BlockSpec(memory_space=pltpu.SMEM)


def pack_kernel(parts, heads, plan_ref, q_ref, k_ref, v_ref, ids_ref, kv_out, send_out, keep_out, meta_out):
    rows = q_ref.shape[0]
    piece = rows // parts
    own = lax.rem(lax.axis_index("head"), 2)
    lane = lax.rem(lax.broadcasted_iota(jnp.int32, (1, rows), 1), rows // 2)
    source = jnp.zeros((1, rows), jnp.int32)
    for a in range(parts // 2):
        for out_ref, parity in ((keep_out, own), (send_out, 1 - own)):
            p = plan_ref[0, 2 * a + parity]
            for h in range(heads):
                at = h * rows // 2 + a * piece
                out_ref[at : at + piece, :] = q_ref[
                    pl.ds(pl.multiple_of(p * piece, piece), piece),
                    h * HEAD_DIM : (h + 1) * HEAD_DIM,
                ]
        p = plan_ref[0, 2 * a + own]
        inside = (lane >= a * piece) & (lane < (a + 1) * piece)
        source = jnp.where(inside, (p - a) * piece + lane, source)
    ids = ids_ref[...].astype(jnp.float32)
    ids_rows = jnp.broadcast_to(ids, (META, rows))
    for b in range(parts):
        kv_out[b, :rows, :] = k_ref[...]
        kv_out[b, rows : 2 * rows, :] = v_ref[...]
        kv_out[b, 2 * rows :, :] = ids_rows.astype(jnp.bfloat16)
    from_row = lax.broadcasted_iota(jnp.int32, (rows, rows), 0)
    chosen = (from_row == source).astype(jnp.float32)
    ids_moved = jnp.dot(ids_rows, chosen, preferred_element_type=jnp.float32)
    row = lax.broadcasted_iota(jnp.int32, (META, rows), 0)
    positions = jnp.broadcast_to(source.astype(jnp.float32), (META, rows))
    meta_out[...] = jnp.where(row == 0, ids_moved, positions)


def attend_kernel(heads, scale, keep_ref, got_ref, kv_ref, kv_pair_ref, meta_ref, out_ref):
    parts = kv_ref.shape[0]
    rows = (kv_ref.shape[1] - META) // 2
    piece = rows // parts
    d = lax.axis_index("ctx")
    turned = meta_ref[...].T
    q_ids, q_pos = turned[:, 0:1], turned[:, 1:2]

    def ids_of(block):
        return kv_ref[block, 2 * rows :, :].astype(jnp.float32)[0:1]

    first_id = jnp.min(ids_of(d))
    start = jnp.int32(0)
    for b in range(parts):
        start = start + (jnp.max(ids_of(b)) < first_id).astype(jnp.int32)
    b0 = lax.div(start, 2) * 2
    tiles = lax.div(d, 2) + 1 - lax.div(start, 2)
    for w in range(1, parts // 2 + 1):

        @pl.when(tiles == w)
        def _(w=w):
            span = 2 * w * rows
            k_ids = jnp.concatenate([ids_of(b0 + n) for n in range(2 * w)], axis=1)
            k_pos = lax.broadcasted_iota(jnp.int32, (1, span), 1) + (b0 - d) * rows
            allowed = (k_ids == q_ids) & (k_pos.astype(jnp.float32) <= q_pos)
            bias = jnp.where(allowed, 0.0, NEG_FILL)
            for side, (q_ref, side_kv) in enumerate(((keep_ref, kv_ref), (got_ref, kv_pair_ref))):
                keys = side_kv[pl.ds(b0, 2 * w), :rows, :].reshape(span, HEAD_DIM)
                vals = side_kv[pl.ds(b0, 2 * w), rows : 2 * rows, :].reshape(span, HEAD_DIM)
                vals = jnp.concatenate([vals, jnp.ones((span, HEAD_DIM), jnp.bfloat16)], axis=1)
                for t in range(heads // 2):
                    q = q_ref[t * rows : (t + 1) * rows, :]
                    s = lax.dot_general(
                        q, keys, (((1,), (1,)), ((), ())), preferred_element_type=jnp.float32
                    )
                    s = s + bias
                    top = jnp.max(s, axis=1, keepdims=True)
                    e = jnp.exp2((s - top) * (scale * math.log2(math.e)))
                    o = jnp.dot(e.astype(jnp.bfloat16), vals, preferred_element_type=jnp.float32)
                    o = (o[:, :HEAD_DIM] / o[:, HEAD_DIM:]).astype(jnp.bfloat16)
                    for n in range(2):
                        col = (side * heads + 2 * t + n) * HEAD_DIM
                        for a in range(parts // 2):
                            at = n * rows // 2 + a * piece
                            out_ref[a, :, col : col + HEAD_DIM] = o[at : at + piece, :]


def project_kernel(group, half, wave, parts, *refs):
    count = parts // 2
    blocks, refs = refs[:count], refs[count:]
    w_ref, w_pair_ref, refs = refs[0], refs[1], refs[2:]
    out_refs, (x_held, w_held, total, sems) = refs[:count], refs[count:]
    depth = w_ref.shape[0]
    me = lax.axis_index("ctx")
    copies = [
        pltpu.make_async_copy(w_ref, w_held.at[:depth], sems.at[count]),
        pltpu.make_async_copy(w_pair_ref, w_held.at[depth:], sems.at[count + 1]),
    ] + [
        pltpu.make_async_copy(
            blocks[k], x_held.at[:, jnp.bitwise_xor(lax.rem(me, count), k)], sems.at[k]
        )
        for k in range(count)
    ]
    for copy in copies:
        copy.start()
    for copy in copies:
        copy.wait()
    rows = total.shape[0]
    x = x_held[...].reshape(rows, 2 * depth)
    total[...] = jnp.dot(x, w_held[...], preferred_element_type=jnp.float32)
    mine = lax.rem(me, group) * half + lax.div(lax.axis_index("head"), 2)
    for k, out_ref in enumerate(out_refs):
        each = rows // count
        at = pl.ds(pl.multiple_of(jnp.bitwise_xor(mine, k) * each, each), each)
        out_ref[...] = total[at, :].astype(jnp.bfloat16)


def final_kernel(group, half, parts, *refs):
    blocks, out_ref = refs[:-1], refs[-1]
    count = len(blocks) // 2
    rows, cols = blocks[0].shape
    high = lax.div(lax.axis_index("ctx"), 2)
    upper = lax.div(lax.axis_index("head") * group, parts // 2)
    for wave in range(2):
        at = pl.ds(pl.multiple_of(lax.rem(upper + wave, 2) * rows, rows), rows)
        for first in range(0, count, half):
            part = lax.div(jnp.bitwise_xor(high, first), half)
            total = blocks[wave * count + first][...].astype(jnp.float32)
            for k in range(first + 1, first + half):
                total = total + blocks[wave * count + k][...].astype(jnp.float32)
            out_ref[at, pl.ds(pl.multiple_of(part * cols, cols), cols)] = total.astype(jnp.bfloat16)


def along_ctx(x, parts, k):
    return lax.ppermute(x, "ctx", [(i, i ^ k) for i in range(parts)])


def spread_over_ctx(block, parts):
    half = parts // 2
    got = {0: block}
    got[half] = along_ctx(block, parts, half)
    for k in [*range(2, half, 2), 1]:
        got[k] = along_ctx(block, parts, k)
    names = sorted(got)
    held = dict(zip(names, lax.optimization_barrier([got[k] for k in names])))
    for k in range(2, half, 2):
        got[half + k] = along_ctx(held[half], parts, k)
    for k in range(2, half + 1, 2):
        got[k + 1] = along_ctx(held[k], parts, 1)
    for k in range(half + 2, parts, 2):
        got[k + 1] = along_ctx(got[k], parts, 1)
    return [got[k] for k in range(parts)]


def packed_body(groups, queries, keys, values, doc_ids, plan, w_out):
    parts = lax.axis_size("ctx")
    rows = queries.shape[0]
    heads = queries.shape[1] // HEAD_DIM
    depth, width = w_out.shape
    group, half = parts // groups, groups // 2
    count, piece = parts // 2, rows // parts
    bf16 = jnp.bfloat16
    params = pltpu.CompilerParams(vmem_limit_bytes=VMEM_LIMIT)
    pair = [(g, g ^ 1) for g in range(groups)]
    kv_rows = 2 * rows + META
    w_pair = lax.ppermute(w_out, "head", pair)
    kv_copies, q_send, q_keep, meta = pl.pallas_call(
        functools.partial(pack_kernel, parts, heads),
        out_shape=[
            jax.ShapeDtypeStruct((parts, kv_rows, HEAD_DIM), bf16),
            jax.ShapeDtypeStruct((heads * rows // 2, HEAD_DIM), bf16),
            jax.ShapeDtypeStruct((heads * rows // 2, HEAD_DIM), bf16),
            jax.ShapeDtypeStruct((META, rows), jnp.float32),
        ],
        in_specs=[SMEM, VMEM, VMEM, VMEM, VMEM],
        out_specs=[VMEM] * 4,
        compiler_params=params,
        name="pack",
    )(plan, queries, keys, values, doc_ids.reshape(1, rows))
    q_got = lax.ppermute(q_send, "head", pair)
    kv = lax.all_to_all(kv_copies, "ctx", split_axis=0, concat_axis=0, tiled=True)
    kv_pair = lax.ppermute(kv, "head", pair)
    attended = pl.pallas_call(
        functools.partial(attend_kernel, heads, 1.0 / math.sqrt(HEAD_DIM)),
        out_shape=jax.ShapeDtypeStruct((count, piece, 2 * depth), bf16),
        in_specs=[VMEM] * 5,
        out_specs=VMEM,
        compiler_params=params,
        name="attend",
    )(q_keep, q_got, kv, kv_pair, meta)
    blocks = spread_over_ctx(attended, parts)
    arrived = []
    for wave in range(2):
        sums = pl.pallas_call(
            functools.partial(project_kernel, group, half, wave, parts),
            out_shape=[jax.ShapeDtypeStruct((rows // 2, width), bf16)] * count,
            in_specs=[ANY] * (count + 2),
            out_specs=[VMEM] * count,
            scratch_shapes=[
                pltpu.VMEM((count, count, piece, 2 * depth), bf16),
                pltpu.VMEM((2 * depth, width), bf16),
                pltpu.VMEM((count * rows // 2, width), jnp.float32),
                pltpu.SemaphoreType.DMA((count + 2,)),
            ],
            compiler_params=params,
            name="project",
        )(*blocks[wave * count : (wave + 1) * count], w_out, w_pair)
        for k in range(count):
            pairs = []
            for c in range(parts):
                for g in range(groups):
                    high = ((c % group) * half + g // 2) ^ k
                    pairs.append((c * groups + g, (high * 2 + g % 2) * groups + c // group))
            arrived.append(lax.ppermute(sums[k], ("ctx", "head"), pairs))
    return pl.pallas_call(
        functools.partial(final_kernel, group, half, parts),
        out_shape=jax.ShapeDtypeStruct((rows, group * width), bf16),
        in_specs=[VMEM] * (2 * count),
        out_specs=VMEM,
        compiler_params=params,
        name="final_sum",
    )(*arrived)


def spread_rows(block, order, parts):
    shaped = block.reshape(parts, block.shape[0] // parts, block.shape[1])
    return jnp.take(shaped, order, axis=0).reshape(block.shape)


def attend(query_rows, row_pos, row_start, all_keys, all_values):
    n_rows = query_rows.shape[0]
    kv_local = all_keys.shape[1] // HEAD_DIM
    group_size = query_rows.shape[1] // all_keys.shape[1]
    q_heads = query_rows.reshape(n_rows, kv_local, group_size, HEAD_DIM).transpose(1, 0, 2, 3)
    q_heads = q_heads.reshape(kv_local, n_rows * group_size, HEAD_DIM)
    pos_rows = jnp.repeat(row_pos, group_size)
    start_rows = jnp.repeat(row_start, group_size)
    q_block = min(n_rows, max(1, 512 // group_size))
    block_rows = q_block * group_size
    n_qblocks = n_rows // q_block
    score_scale = 1.0 / math.sqrt(HEAD_DIM)
    total_keys = all_keys.shape[0]
    key_size = math.gcd(total_keys, 512)
    n_kblocks = total_keys // key_size
    key_tiles = all_keys.reshape(n_kblocks, key_size, kv_local, HEAD_DIM)
    value_tiles = all_values.reshape(n_kblocks, key_size, kv_local, HEAD_DIM)
    initial = (
        jnp.full((kv_local, n_rows * group_size), NEG_FILL, jnp.float32),
        jnp.zeros((kv_local, n_rows * group_size), jnp.float32),
        jnp.zeros((kv_local, n_rows * group_size, HEAD_DIM), jnp.float32),
    )

    def one_query_block(block_index, state):
        run_max, run_sum, run_acc = state
        offset = block_index * block_rows
        q_part = lax.dynamic_slice_in_dim(q_heads, offset, block_rows, 1)
        pos_part = lax.dynamic_slice_in_dim(pos_rows, offset, block_rows, 0)
        start_part = lax.dynamic_slice_in_dim(start_rows, offset, block_rows, 0)
        first_block = jnp.clip(jnp.min(start_part) // key_size, 0, n_kblocks)
        last_block = jnp.clip(jnp.max(pos_part) // key_size + 1, 0, n_kblocks)

        def add_tile(key_index, inner):
            block_max, block_sum, block_acc = inner
            key_tile = lax.dynamic_index_in_dim(key_tiles, key_index, 0, keepdims=False)
            value_tile = lax.dynamic_index_in_dim(value_tiles, key_index, 0, keepdims=False)
            scores = (
                jnp.einsum("grd,kgd->grk", q_part, key_tile, preferred_element_type=jnp.float32)
                * score_scale
            )
            key_pos = key_index * key_size + jnp.arange(key_size, dtype=jnp.int32)
            allowed = (key_pos[None, :] >= start_part[:, None]) & (
                key_pos[None, :] <= pos_part[:, None]
            )
            scores = jnp.where(allowed[None], scores, NEG_FILL)
            new_max = jnp.maximum(block_max, jnp.max(scores, axis=-1))
            expo = jnp.where(allowed[None], jnp.exp(scores - new_max[..., None]), 0.0)
            rescale = jnp.exp(block_max - new_max)
            block_sum = block_sum * rescale + jnp.sum(expo, axis=-1)
            block_acc = block_acc * rescale[..., None] + jnp.einsum(
                "grk,kgd->grd",
                expo.astype(jnp.bfloat16),
                value_tile,
                preferred_element_type=jnp.float32,
            )
            return (new_max, block_sum, block_acc)

        def one_key_block(key_index, inner):
            tile_low = key_index * key_size
            tile_high = tile_low + key_size - 1
            meets = jnp.any((start_part <= tile_high) & (pos_part >= tile_low))
            return lax.cond(
                meets, lambda carried: add_tile(key_index, carried), lambda carried: carried, inner
            )

        inner = (
            lax.dynamic_slice_in_dim(run_max, offset, block_rows, 1),
            lax.dynamic_slice_in_dim(run_sum, offset, block_rows, 1),
            lax.dynamic_slice_in_dim(run_acc, offset, block_rows, 1),
        )
        new_max, new_sum, new_acc = lax.fori_loop(first_block, last_block, one_key_block, inner)
        run_max = lax.dynamic_update_slice_in_dim(run_max, new_max, offset, 1)
        run_sum = lax.dynamic_update_slice_in_dim(run_sum, new_sum, offset, 1)
        run_acc = lax.dynamic_update_slice_in_dim(run_acc, new_acc, offset, 1)
        return (run_max, run_sum, run_acc)

    final_max, final_sum, final_acc = lax.fori_loop(0, n_qblocks, one_query_block, initial)
    result = final_acc / final_sum[..., None]
    result = result.reshape(kv_local, n_rows, group_size, HEAD_DIM).transpose(1, 0, 2, 3)
    return result.reshape(n_rows, kv_local * group_size * HEAD_DIM).astype(jnp.bfloat16)


def body(queries, keys, values, doc_ids, plan, w_out):
    n_rows = queries.shape[0]
    parts = lax.axis_size("ctx")
    my_index = lax.axis_index("ctx")
    all_ids, all_plan = (
        lax.all_gather(doc_ids, "ctx", axis=0, tiled=True),
        lax.all_gather(plan, "ctx", axis=0, tiled=True),
    )
    all_keys, all_values = (
        lax.all_gather(keys, "ctx", axis=0, tiled=True),
        lax.all_gather(values, "ctx", axis=0, tiled=True),
    )
    doc_range = jnp.arange(DOCS, dtype=jnp.int32)
    doc_first = jnp.sum((all_ids[None, :] < doc_range[:, None]).astype(jnp.int32), axis=1)
    local_pos = my_index * n_rows + jnp.arange(n_rows, dtype=jnp.int32)
    ids_here = jnp.take(all_ids, local_pos)
    local_out = attend(
        queries,
        local_pos,
        jnp.sum(jnp.where(ids_here[:, None] == doc_range[None, :], doc_first[None, :], 0), axis=1),
        all_keys,
        all_values,
    )
    attended = lax.all_to_all(
        spread_rows(local_out, plan[0], parts), "ctx", split_axis=0, concat_axis=0, tiled=True
    )
    stacked = jnp.dot(
        lax.all_gather(attended, "ctx", axis=0, tiled=True),
        w_out,
        preferred_element_type=jnp.float32,
    )
    partial_sum = lax.all_to_all(
        stacked.astype(jnp.bfloat16), "ctx", split_axis=0, concat_axis=1, tiled=True
    ).astype(stacked.dtype)
    summed = lax.psum_scatter(
        partial_sum.astype(jnp.bfloat16), "head", scatter_dimension=1, tiled=True
    )
    return summed


def fits(parts, groups, rows, width):
    powers = all(n & (n - 1) == 0 for n in (parts, groups))
    window = parts * rows * width * 2
    whole = rows % (16 * parts) == 0 and groups % 2 == 0 and parts % groups == 0
    return powers and whole and 8 * window <= VMEM_LIMIT


def solution(mesh):
    parts, groups = mesh.shape["ctx"], mesh.shape["head"]

    def one_device(queries, keys, values, doc_ids, plan, w_out):
        one_pair = keys.shape[1] == HEAD_DIM
        if one_pair and fits(parts, groups, queries.shape[0], queries.shape[1]):
            return packed_body(groups, queries, keys, values, doc_ids, plan, w_out)
        return body(queries, keys, values, doc_ids, plan, w_out)

    return jax.shard_map(
        one_device,
        mesh=mesh,
        in_specs=(
            P("ctx", "head"),
            P("ctx", "head"),
            P("ctx", "head"),
            P("ctx"),
            P("ctx", None),
            P("head", "ctx"),
        ),
        out_specs=P("ctx", "head"),
        check_vma=False,
    )
```

```python
import functools
import math

import jax
import jax.numpy as jnp
from jax import lax
from jax.experimental import pallas as pl
from jax.experimental.pallas import tpu as pltpu
from jax.sharding import PartitionSpec as P

HEAD_DIM = 128
DOCS = 16
META = 16
NEG_FILL = -1e30
VMEM_LIMIT = 24 * 1024 * 1024
PACK_LIMIT = 56 * 1024 * 1024

ANY = pl.BlockSpec(memory_space=pl.ANY)
VMEM = pl.BlockSpec(memory_space=pltpu.VMEM)
SMEM = pl.BlockSpec(memory_space=pltpu.SMEM)


def pack_kernel(parts, heads, plan_ref, q_ref, k_ref, v_ref, ids_ref, all_out, q_out, kv_out):
    rows = q_ref.shape[0]
    piece = rows // parts
    lane = lax.broadcasted_iota(jnp.int32, (1, rows), 1)
    source = jnp.zeros((1, rows), jnp.int32)
    for j in range(parts):
        p = plan_ref[0, j]
        for h in range(heads):
            moved = q_ref[
                pl.ds(pl.multiple_of(p * piece, piece), piece), h * HEAD_DIM : (h + 1) * HEAD_DIM
            ]
            q_out[h * rows + j * piece : h * rows + (j + 1) * piece, :] = moved
            all_out[h * rows + j * piece : h * rows + (j + 1) * piece, :] = moved
        source = jnp.where(
            (lane >= j * piece) & (lane < (j + 1) * piece), (p - j) * piece + lane, source
        )
    ids = ids_ref[...].astype(jnp.float32)
    row = lax.broadcasted_iota(jnp.int32, (META, rows), 0)
    from_row = lax.broadcasted_iota(jnp.int32, (rows, rows), 0)
    chosen = (from_row == source).astype(jnp.float32)
    ids_rows = jnp.broadcast_to(ids, (META, rows))
    ids_moved = jnp.dot(ids_rows, chosen, preferred_element_type=jnp.float32)
    positions = jnp.broadcast_to(source.astype(jnp.float32), (META, rows))
    meta = jnp.where(row == 0, ids_rows, jnp.where(row == 1, ids_moved, positions))
    for out_ref, base in ((all_out, heads * rows), (kv_out, 0)):
        out_ref[base : base + rows, :] = k_ref[...]
        out_ref[base + rows : base + 2 * rows, :] = v_ref[...]
        out_ref[base + 2 * rows :, :] = meta.astype(jnp.bfloat16)


def attend_kernel(parts, heads, scale, wave, *refs):
    half = parts // 2
    near, far, refs = refs[:half], refs[half : 2 * half], refs[2 * half :]
    q_blocks = near
    if wave:
        q_blocks, refs = refs[:half], refs[half:]
    send_ref, keep_ref, q_held, kv_held, vals_ref, rows_ref, ends, sems = refs
    rows = q_held.shape[1] // heads
    piece = rows // parts
    me = lax.axis_index("ctx")
    other = 1 - lax.rem(lax.axis_index("head"), 2)
    first_block = half * lax.rem(lax.div(me, half) + wave, 2)
    q_rows = heads * rows
    kv_copies = [
        pltpu.make_async_copy(
            near[k].at[q_rows:], kv_held.at[jnp.bitwise_xor(me, k)], sems.at[half + k]
        )
        for k in range(half)
    ] + [
        pltpu.make_async_copy(
            far[k], kv_held.at[jnp.bitwise_xor(me, half + k)], sems.at[2 * half + k]
        )
        for k in range(half)
    ]
    copies = [
        pltpu.make_async_copy(
            q_blocks[k].at[:q_rows], q_held.at[jnp.bitwise_xor(lax.rem(me, half), k)], sems.at[k]
        )
        for k in range(half)
    ]
    for copy in kv_copies + copies:
        copy.start()
    for copy in kv_copies:
        copy.wait()

    def ids_of(block):
        return kv_held[block, 2 * rows :, :].astype(jnp.float32)

    for b in range(parts):
        vals_ref[b, :, :HEAD_DIM] = kv_held[b, rows : 2 * rows, :]
        vals_ref[b, :, HEAD_DIM:] = jnp.ones((rows, HEAD_DIM), jnp.bfloat16)
        ids = ids_of(b)[0:1]
        ends[0, b] = jnp.min(ids)
        ends[1, b] = jnp.max(ids)

    for copy in copies:
        copy.wait()

    def one_block(i, carry):
        d = first_block + i
        turned = ids_of(d).T
        q_ids, q_pos = turned[:, 1:2], turned[:, 2:3]
        start = jnp.int32(0)
        for b in range(parts):
            start = start + (ends[1, b] < ends[0, d]).astype(jnp.int32)
        b0 = lax.div(start, 2) * 2
        tiles = lax.div(d, 2) + 1 - lax.div(start, 2)
        for w in range(1, half + 1):

            @pl.when(tiles == w)
            def _(w=w):
                span = 2 * w * rows
                k_ids = jnp.concatenate([ids_of(b0 + n)[0:1] for n in range(2 * w)], axis=1)
                k_pos = lax.broadcasted_iota(jnp.int32, (1, span), 1) + (b0 - d) * rows
                allowed = (k_ids == q_ids) & (k_pos.astype(jnp.float32) <= q_pos)
                bias = jnp.where(allowed, 0.0, NEG_FILL)
                keys = kv_held[pl.ds(b0, 2 * w), :rows, :].reshape(span, HEAD_DIM)
                vals = vals_ref[pl.ds(b0, 2 * w), :, :].reshape(span, 2 * HEAD_DIM)
                for h in range(heads):
                    q = q_held[i, h * rows : (h + 1) * rows, :]
                    s = lax.dot_general(
                        q, keys, (((1,), (1,)), ((), ())), preferred_element_type=jnp.float32
                    )
                    s = s + bias
                    top = jnp.max(s, axis=1, keepdims=True)
                    e = jnp.exp2((s - top) * (scale * math.log2(math.e)))
                    o = jnp.dot(e.astype(jnp.bfloat16), vals, preferred_element_type=jnp.float32)
                    o = (o[:, :HEAD_DIM] / o[:, HEAD_DIM:]).astype(jnp.bfloat16)
                    for j in range(parts):
                        at = pl.multiple_of((j // 2) * half * piece + i * piece, piece)
                        rows_ref[
                            jnp.bitwise_xor(other, j % 2),
                            pl.ds(at, piece),
                            h * HEAD_DIM : (h + 1) * HEAD_DIM,
                        ] = o[j * piece : (j + 1) * piece, :]

        return carry

    lax.fori_loop(0, half, one_block, 0)
    out = [
        pltpu.make_async_copy(rows_ref.at[0], send_ref, sems.at[0]),
        pltpu.make_async_copy(rows_ref.at[1], keep_ref, sems.at[1]),
    ]
    for copy in out:
        copy.start()
    for copy in out:
        copy.wait()


def project_kernel(group, half, *refs):
    (keep_0, got_0, keep_1, got_1, w_ref, w_pair_ref), refs = refs[:6], refs[6:]
    out_refs, total = refs[:-1], refs[-1]
    count = len(out_refs)
    rows = keep_0.shape[0] // count
    me = lax.axis_index("ctx")
    upper = lax.div(me, count)
    mine = lax.rem(me, group) * half + lax.div(lax.axis_index("head"), 2)
    for wave, keep_ref, got_ref in ((0, keep_0, got_0), (1, keep_1, got_1)):
        total[...] = jnp.dot(
            keep_ref[...], w_ref[...], preferred_element_type=jnp.float32
        ) + jnp.dot(got_ref[...], w_pair_ref[...], preferred_element_type=jnp.float32)
        place = pl.ds(pl.multiple_of(lax.rem(upper + wave, 2) * rows, rows), rows)
        for k, out_ref in enumerate(out_refs):
            at = pl.ds(pl.multiple_of(jnp.bitwise_xor(mine, k) * rows, rows), rows)
            out_ref[place, :] = total[at, :].astype(jnp.bfloat16)


def final_kernel(group, half, *refs):
    blocks, out_ref = refs[:-1], refs[-1]
    cols = blocks[0].shape[1]
    high = lax.div(lax.axis_index("ctx"), 2)
    for first in range(0, len(blocks), half):
        part = lax.div(jnp.bitwise_xor(high, first), half)
        total = blocks[first][...].astype(jnp.float32)
        for k in range(first + 1, first + half):
            total = total + blocks[k][...].astype(jnp.float32)
        out_ref[:, pl.ds(pl.multiple_of(part * cols, cols), cols)] = total.astype(jnp.bfloat16)


def along_ctx(x, parts, k):
    return lax.ppermute(x, "ctx", [(i, i ^ k) for i in range(parts)])


def spread_over_ctx(block, q_block, kv_block, parts):
    half = parts // 2
    near, far_q, far_kv = {0: block}, {}, {}
    far_q[0] = along_ctx(q_block, parts, half)
    for k in [*range(2, half, 2), 1]:
        near[k] = along_ctx(block, parts, k)
    far_kv[0] = along_ctx(kv_block, parts, half)
    far_kv[1] = along_ctx(kv_block, parts, half + 1)
    near, far_q, far_kv = lax.optimization_barrier((near, far_q, far_kv))
    for k in range(2, half, 2):
        near[k + 1] = along_ctx(near[k], parts, 1)
        far_q[k] = along_ctx(far_q[0], parts, k)
        far_kv[k] = along_ctx(far_kv[0], parts, k)
        far_kv[k + 1] = along_ctx(far_kv[1], parts, k)
    far_q[1] = along_ctx(far_q[0], parts, 1)
    near, far_q, far_kv = lax.optimization_barrier((near, far_q, far_kv))
    for k in range(2, half, 2):
        far_q[k + 1] = along_ctx(far_q[k], parts, 1)
    return [[some[k] for k in range(half)] for some in (near, far_q, far_kv)]


def packed_body(groups, queries, keys, values, doc_ids, plan, w_out):
    parts = lax.axis_size("ctx")
    rows = queries.shape[0]
    heads = queries.shape[1] // HEAD_DIM
    width = w_out.shape[1]
    group, half = parts // groups, groups // 2
    bf16 = jnp.bfloat16
    params = pltpu.CompilerParams(vmem_limit_bytes=VMEM_LIMIT)
    pair = [(g, g ^ 1) for g in range(groups)]
    kv_rows = 2 * rows + META
    w_pair = lax.ppermute(w_out, "head", pair)
    block, q_block, kv_block = pl.pallas_call(
        functools.partial(pack_kernel, parts, heads),
        out_shape=[
            jax.ShapeDtypeStruct((heads * rows + kv_rows, HEAD_DIM), bf16),
            jax.ShapeDtypeStruct((heads * rows, HEAD_DIM), bf16),
            jax.ShapeDtypeStruct((kv_rows, HEAD_DIM), bf16),
        ],
        in_specs=[SMEM, VMEM, VMEM, VMEM, VMEM],
        out_specs=[VMEM] * 3,
        compiler_params=pltpu.CompilerParams(vmem_limit_bytes=PACK_LIMIT),
        name="pack",
    )(plan, queries, keys, values, doc_ids.reshape(1, rows))
    near, far_q, far_kv = spread_over_ctx(block, q_block, kv_block, parts)
    wave_rows = parts * rows // 4
    count = parts // 2
    arrived, halves = [], []
    for wave in range(2):
        inputs = [*near, *far_kv]
        if wave:
            inputs = inputs + far_q
        send, keep = pl.pallas_call(
            functools.partial(attend_kernel, parts, heads, 1.0 / math.sqrt(HEAD_DIM), wave),
            out_shape=[jax.ShapeDtypeStruct((wave_rows, heads * HEAD_DIM), bf16)] * 2,
            in_specs=[ANY] * len(inputs),
            out_specs=[ANY, ANY],
            scratch_shapes=[
                pltpu.VMEM((count, heads * rows, HEAD_DIM), bf16),
                pltpu.VMEM((parts, kv_rows, HEAD_DIM), bf16),
                pltpu.VMEM((parts, rows, 2 * HEAD_DIM), bf16),
                pltpu.VMEM((2, wave_rows, heads * HEAD_DIM), bf16),
                pltpu.SMEM((2, parts), jnp.float32),
                pltpu.SemaphoreType.DMA((count + parts,)),
            ],
            compiler_params=params,
            cost_estimate=pl.CostEstimate(flops=8 * 10**9, bytes_accessed=2**22, transcendentals=0),
            name="attend",
        )(*inputs)
        halves += [keep, lax.ppermute(send, "head", pair)]
    sums = pl.pallas_call(
        functools.partial(project_kernel, group, half),
        out_shape=[jax.ShapeDtypeStruct((rows, width), bf16)] * count,
        in_specs=[VMEM] * 6,
        out_specs=[VMEM] * count,
        scratch_shapes=[pltpu.VMEM((wave_rows, width), jnp.float32)],
        compiler_params=params,
        name="project",
    )(*halves, w_out, w_pair)
    for k in range(count):
        pairs = []
        for c in range(parts):
            for g in range(groups):
                high = ((c % group) * half + g // 2) ^ k
                pairs.append((c * groups + g, (high * 2 + g % 2) * groups + c // group))
        arrived.append(lax.ppermute(sums[k], ("ctx", "head"), pairs))
    return pl.pallas_call(
        functools.partial(final_kernel, group, half),
        out_shape=jax.ShapeDtypeStruct((rows, group * width), bf16),
        in_specs=[VMEM] * count,
        out_specs=VMEM,
        compiler_params=params,
        name="final_sum",
    )(*arrived)


def spread_rows(block, order, parts):
    shaped = block.reshape(parts, block.shape[0] // parts, block.shape[1])
    return jnp.take(shaped, order, axis=0).reshape(block.shape)


def attend(query_rows, row_pos, row_start, all_keys, all_values):
    n_rows = query_rows.shape[0]
    kv_local = all_keys.shape[1] // HEAD_DIM
    group_size = query_rows.shape[1] // all_keys.shape[1]
    q_heads = query_rows.reshape(n_rows, kv_local, group_size, HEAD_DIM).transpose(1, 0, 2, 3)
    q_heads = q_heads.reshape(kv_local, n_rows * group_size, HEAD_DIM)
    pos_rows = jnp.repeat(row_pos, group_size)
    start_rows = jnp.repeat(row_start, group_size)
    q_block = min(n_rows, max(1, 512 // group_size))
    block_rows = q_block * group_size
    n_qblocks = n_rows // q_block
    score_scale = 1.0 / math.sqrt(HEAD_DIM)
    total_keys = all_keys.shape[0]
    key_size = math.gcd(total_keys, 512)
    n_kblocks = total_keys // key_size
    key_tiles = all_keys.reshape(n_kblocks, key_size, kv_local, HEAD_DIM)
    value_tiles = all_values.reshape(n_kblocks, key_size, kv_local, HEAD_DIM)
    initial = (
        jnp.full((kv_local, n_rows * group_size), NEG_FILL, jnp.float32),
        jnp.zeros((kv_local, n_rows * group_size), jnp.float32),
        jnp.zeros((kv_local, n_rows * group_size, HEAD_DIM), jnp.float32),
    )

    def one_query_block(block_index, state):
        run_max, run_sum, run_acc = state
        offset = block_index * block_rows
        q_part = lax.dynamic_slice_in_dim(q_heads, offset, block_rows, 1)
        pos_part = lax.dynamic_slice_in_dim(pos_rows, offset, block_rows, 0)
        start_part = lax.dynamic_slice_in_dim(start_rows, offset, block_rows, 0)
        first_block = jnp.clip(jnp.min(start_part) // key_size, 0, n_kblocks)
        last_block = jnp.clip(jnp.max(pos_part) // key_size + 1, 0, n_kblocks)

        def add_tile(key_index, inner):
            block_max, block_sum, block_acc = inner
            key_tile = lax.dynamic_index_in_dim(key_tiles, key_index, 0, keepdims=False)
            value_tile = lax.dynamic_index_in_dim(value_tiles, key_index, 0, keepdims=False)
            scores = (
                jnp.einsum("grd,kgd->grk", q_part, key_tile, preferred_element_type=jnp.float32)
                * score_scale
            )
            key_pos = key_index * key_size + jnp.arange(key_size, dtype=jnp.int32)
            allowed = (key_pos[None, :] >= start_part[:, None]) & (
                key_pos[None, :] <= pos_part[:, None]
            )
            scores = jnp.where(allowed[None], scores, NEG_FILL)
            new_max = jnp.maximum(block_max, jnp.max(scores, axis=-1))
            expo = jnp.where(allowed[None], jnp.exp(scores - new_max[..., None]), 0.0)
            rescale = jnp.exp(block_max - new_max)
            block_sum = block_sum * rescale + jnp.sum(expo, axis=-1)
            block_acc = block_acc * rescale[..., None] + jnp.einsum(
                "grk,kgd->grd",
                expo.astype(jnp.bfloat16),
                value_tile,
                preferred_element_type=jnp.float32,
            )
            return (new_max, block_sum, block_acc)

        def one_key_block(key_index, inner):
            tile_low = key_index * key_size
            tile_high = tile_low + key_size - 1
            meets = jnp.any((start_part <= tile_high) & (pos_part >= tile_low))
            return lax.cond(
                meets, lambda carried: add_tile(key_index, carried), lambda carried: carried, inner
            )

        inner = (
            lax.dynamic_slice_in_dim(run_max, offset, block_rows, 1),
            lax.dynamic_slice_in_dim(run_sum, offset, block_rows, 1),
            lax.dynamic_slice_in_dim(run_acc, offset, block_rows, 1),
        )
        new_max, new_sum, new_acc = lax.fori_loop(first_block, last_block, one_key_block, inner)
        run_max = lax.dynamic_update_slice_in_dim(run_max, new_max, offset, 1)
        run_sum = lax.dynamic_update_slice_in_dim(run_sum, new_sum, offset, 1)
        run_acc = lax.dynamic_update_slice_in_dim(run_acc, new_acc, offset, 1)
        return (run_max, run_sum, run_acc)

    final_max, final_sum, final_acc = lax.fori_loop(0, n_qblocks, one_query_block, initial)
    result = final_acc / final_sum[..., None]
    result = result.reshape(kv_local, n_rows, group_size, HEAD_DIM).transpose(1, 0, 2, 3)
    return result.reshape(n_rows, kv_local * group_size * HEAD_DIM).astype(jnp.bfloat16)


def body(queries, keys, values, doc_ids, plan, w_out):
    n_rows = queries.shape[0]
    parts = lax.axis_size("ctx")
    my_index = lax.axis_index("ctx")
    all_ids, all_plan = (
        lax.all_gather(doc_ids, "ctx", axis=0, tiled=True),
        lax.all_gather(plan, "ctx", axis=0, tiled=True),
    )
    all_keys, all_values = (
        lax.all_gather(keys, "ctx", axis=0, tiled=True),
        lax.all_gather(values, "ctx", axis=0, tiled=True),
    )
    doc_range = jnp.arange(DOCS, dtype=jnp.int32)
    doc_first = jnp.sum((all_ids[None, :] < doc_range[:, None]).astype(jnp.int32), axis=1)
    local_pos = my_index * n_rows + jnp.arange(n_rows, dtype=jnp.int32)
    ids_here = jnp.take(all_ids, local_pos)
    local_out = attend(
        queries,
        local_pos,
        jnp.sum(jnp.where(ids_here[:, None] == doc_range[None, :], doc_first[None, :], 0), axis=1),
        all_keys,
        all_values,
    )
    attended = lax.all_to_all(
        spread_rows(local_out, plan[0], parts), "ctx", split_axis=0, concat_axis=0, tiled=True
    )
    stacked = jnp.dot(
        lax.all_gather(attended, "ctx", axis=0, tiled=True),
        w_out,
        preferred_element_type=jnp.float32,
    )
    partial_sum = lax.all_to_all(
        stacked.astype(jnp.bfloat16), "ctx", split_axis=0, concat_axis=1, tiled=True
    ).astype(stacked.dtype)
    summed = lax.psum_scatter(
        partial_sum.astype(jnp.bfloat16), "head", scatter_dimension=1, tiled=True
    )
    return summed


def fits(parts, groups, rows, width):
    powers = all(n & (n - 1) == 0 for n in (parts, groups))
    window = parts * rows * width * 2
    whole = rows % (16 * parts) == 0 and groups % 2 == 0 and parts % groups == 0
    return powers and whole and 8 * window <= VMEM_LIMIT


def solution(mesh):
    parts, groups = mesh.shape["ctx"], mesh.shape["head"]

    def one_device(queries, keys, values, doc_ids, plan, w_out):
        one_pair = keys.shape[1] == HEAD_DIM
        if one_pair and fits(parts, groups, queries.shape[0], queries.shape[1]):
            return packed_body(groups, queries, keys, values, doc_ids, plan, w_out)
        return body(queries, keys, values, doc_ids, plan, w_out)

    return jax.shard_map(
        one_device,
        mesh=mesh,
        in_specs=(
            P("ctx", "head"),
            P("ctx", "head"),
            P("ctx", "head"),
            P("ctx"),
            P("ctx", None),
            P("head", "ctx"),
        ),
        out_specs=P("ctx", "head"),
        check_vma=False,
    )
```

```python
import functools
import math

import jax
import jax.numpy as jnp
from jax import lax
from jax.experimental import pallas as pl
from jax.experimental.pallas import tpu as pltpu
from jax.sharding import PartitionSpec as P

HEAD_DIM = 128
DOCS = 16
META = 16
NEG_FILL = -1e30
VMEM_LIMIT = 24 * 1024 * 1024
PACK_LIMIT = 56 * 1024 * 1024

ANY = pl.BlockSpec(memory_space=pl.ANY)
VMEM = pl.BlockSpec(memory_space=pltpu.VMEM)
SMEM = pl.BlockSpec(memory_space=pltpu.SMEM)


def pack_kernel(parts, heads, plan_ref, q_ref, k_ref, v_ref, ids_ref, all_out, q_out, kv_out):
    rows = q_ref.shape[0]
    piece = rows // parts
    lane = lax.broadcasted_iota(jnp.int32, (1, rows), 1)
    source = jnp.zeros((1, rows), jnp.int32)
    for j in range(parts):
        p = plan_ref[0, j]
        for h in range(heads):
            moved = q_ref[
                pl.ds(pl.multiple_of(p * piece, piece), piece), h * HEAD_DIM : (h + 1) * HEAD_DIM
            ]
            q_out[h * rows + j * piece : h * rows + (j + 1) * piece, :] = moved
            all_out[h * rows + j * piece : h * rows + (j + 1) * piece, :] = moved
        source = jnp.where(
            (lane >= j * piece) & (lane < (j + 1) * piece), (p - j) * piece + lane, source
        )
    ids = ids_ref[...].astype(jnp.float32)
    row = lax.broadcasted_iota(jnp.int32, (META, rows), 0)
    from_row = lax.broadcasted_iota(jnp.int32, (rows, rows), 0)
    chosen = (from_row == source).astype(jnp.float32)
    ids_rows = jnp.broadcast_to(ids, (META, rows))
    ids_moved = jnp.dot(ids_rows, chosen, preferred_element_type=jnp.float32)
    positions = jnp.broadcast_to(source.astype(jnp.float32), (META, rows))
    meta = jnp.where(row == 0, ids_rows, jnp.where(row == 1, ids_moved, positions))
    for out_ref, base in ((all_out, heads * rows), (kv_out, 0)):
        out_ref[base : base + rows, :] = k_ref[...]
        out_ref[base + rows : base + 2 * rows, :] = v_ref[...]
        out_ref[base + 2 * rows :, :] = meta.astype(jnp.bfloat16)


def attend_kernel(parts, heads, scale, slots, *refs):
    half, many = parts // 2, len(slots)
    near, far, refs = refs[:half], refs[half : 2 * half], refs[2 * half :]
    q_blocks = [near[k] for k in slots if k < half]
    if not q_blocks:
        q_blocks, refs = refs[:many], refs[many:]
    send_ref, keep_ref, q_held, kv_held, rows_ref, ends, sems = refs
    rows = q_held.shape[1] // heads
    piece = rows // parts
    me = lax.axis_index("ctx")
    other = 1 - lax.rem(lax.axis_index("head"), 2)
    q_rows = heads * rows
    copies = [
        pltpu.make_async_copy(
            near[k].at[q_rows:], kv_held.at[jnp.bitwise_xor(me, k)], sems.at[half + k]
        )
        for k in range(half)
    ] + [
        pltpu.make_async_copy(
            far[k], kv_held.at[jnp.bitwise_xor(me, half + k)], sems.at[2 * half + k]
        )
        for k in range(half)
    ] + [
        pltpu.make_async_copy(q_blocks[i].at[:q_rows], q_held.at[i], sems.at[i])
        for i in range(many)
    ]
    for copy in copies:
        copy.start()
    for copy in copies:
        copy.wait()

    def ids_of(block):
        return kv_held[block, 2 * rows :, :].astype(jnp.float32)

    for b in range(parts):
        ids = ids_of(b)[0:1]
        ends[0, b] = jnp.min(ids)
        ends[1, b] = jnp.max(ids)

    def one_block(i, carry):
        d = jnp.bitwise_xor(me, slots[0] + i)
        turned = ids_of(d).T
        q_ids, q_pos = turned[:, 1:2], turned[:, 2:3]
        start = jnp.int32(0)
        for b in range(parts):
            start = start + (ends[1, b] < ends[0, d]).astype(jnp.int32)
        b0 = lax.div(start, 2) * 2
        tiles = lax.div(d, 2) + 1 - lax.div(start, 2)
        for w in range(1, half + 1):

            @pl.when(tiles == w)
            def _(w=w):
                span = 2 * w * rows
                k_ids = jnp.concatenate([ids_of(b0 + n)[0:1] for n in range(2 * w)], axis=1)
                k_pos = lax.broadcasted_iota(jnp.int32, (1, span), 1) + (b0 - d) * rows
                allowed = (k_ids == q_ids) & (k_pos.astype(jnp.float32) <= q_pos)
                bias = jnp.where(allowed, 0.0, NEG_FILL)
                keys = kv_held[pl.ds(b0, 2 * w), :rows, :].reshape(span, HEAD_DIM)
                vals = kv_held[pl.ds(b0, 2 * w), rows : 2 * rows, :].reshape(span, HEAD_DIM)
                vals = jnp.concatenate([vals, jnp.ones((span, HEAD_DIM), jnp.bfloat16)], axis=1)
                for h in range(heads):
                    q = q_held[i, h * rows : (h + 1) * rows, :]
                    s = lax.dot_general(
                        q, keys, (((1,), (1,)), ((), ())), preferred_element_type=jnp.float32
                    )
                    s = s + bias
                    top = jnp.max(s, axis=1, keepdims=True)
                    e = jnp.exp2((s - top) * (scale * math.log2(math.e)))
                    o = jnp.dot(e.astype(jnp.bfloat16), vals, preferred_element_type=jnp.float32)
                    o = (o[:, :HEAD_DIM] / o[:, HEAD_DIM:]).astype(jnp.bfloat16)
                    for j in range(parts):
                        at = pl.multiple_of((j // 2) * many * piece + i * piece, piece)
                        rows_ref[
                            jnp.bitwise_xor(other, j % 2),
                            pl.ds(at, piece),
                            h * HEAD_DIM : (h + 1) * HEAD_DIM,
                        ] = o[j * piece : (j + 1) * piece, :]

        return carry

    lax.fori_loop(0, many, one_block, 0)
    out = [
        pltpu.make_async_copy(rows_ref.at[0], send_ref, sems.at[0]),
        pltpu.make_async_copy(rows_ref.at[1], keep_ref, sems.at[1]),
    ]
    for copy in out:
        copy.start()
    for copy in out:
        copy.wait()


def project_kernel(group, half, parts, groups_of_slots, *refs):
    halves, refs = refs[: 2 * len(groups_of_slots)], refs[2 * len(groups_of_slots) :]
    w_ref, w_pair_ref, refs = refs[0], refs[1], refs[2:]
    out_refs, (x_keep, x_got, total) = refs[:-3], refs[-3:]
    count = len(out_refs)
    rows = out_refs[0].shape[0]
    piece = rows // parts
    me = lax.axis_index("ctx")
    for n, slots in enumerate(groups_of_slots):
        for held, part in ((x_keep, halves[2 * n]), (x_got, halves[2 * n + 1])):
            for i, slot in enumerate(slots):
                d = jnp.bitwise_xor(me, slot)
                for a in range(count):
                    at = pl.ds(pl.multiple_of(a * rows + d * piece, piece), piece)
                    first = (a * len(slots) + i) * piece
                    held[at, :] = part[first : first + piece, :]
    total[...] = jnp.dot(x_keep[...], w_ref[...], preferred_element_type=jnp.float32) + jnp.dot(
        x_got[...], w_pair_ref[...], preferred_element_type=jnp.float32
    )
    mine = lax.rem(me, group) * half + lax.div(lax.axis_index("head"), 2)
    for k, out_ref in enumerate(out_refs):
        at = pl.ds(pl.multiple_of(jnp.bitwise_xor(mine, k) * rows, rows), rows)
        out_ref[...] = total[at, :].astype(jnp.bfloat16)


def final_kernel(group, half, *refs):
    blocks, out_ref = refs[:-1], refs[-1]
    cols = blocks[0].shape[1]
    high = lax.div(lax.axis_index("ctx"), 2)
    for first in range(0, len(blocks), half):
        part = lax.div(jnp.bitwise_xor(high, first), half)
        total = blocks[first][...].astype(jnp.float32)
        for k in range(first + 1, first + half):
            total = total + blocks[k][...].astype(jnp.float32)
        out_ref[:, pl.ds(pl.multiple_of(part * cols, cols), cols)] = total.astype(jnp.bfloat16)


def along_ctx(x, parts, k):
    return lax.ppermute(x, "ctx", [(i, i ^ k) for i in range(parts)])


def spread_first(block, q_block, kv_block, parts):
    half = parts // 2
    near, far_kv = {0: block}, {}
    far_kv[0] = along_ctx(kv_block, parts, half)
    far_kv[1] = along_ctx(kv_block, parts, half + 1)
    for k in [*range(2, half, 2), 1]:
        near[k] = along_ctx(block, parts, k)
    far_q = along_ctx(q_block, parts, half)
    near, far_kv = lax.optimization_barrier((near, far_kv))
    for k in range(2, half, 2):
        near[k + 1] = along_ctx(near[k], parts, 1)
        far_kv[k] = along_ctx(far_kv[0], parts, k)
        far_kv[k + 1] = along_ctx(far_kv[1], parts, k)
    return [near[k] for k in range(half)], [far_kv[k] for k in range(half)], far_q


def spread_second(far_q, parts):
    half = parts // 2
    got = {k: along_ctx(far_q, parts, k) for k in [*range(2, half, 2), 1]}
    return lax.optimization_barrier(got)


def spread_third(far_q, got, parts):
    half = parts // 2
    for k in range(2, half, 2):
        got[k + 1] = along_ctx(got[k], parts, 1)
    return [far_q] + [got[k] for k in range(1, half)]


def packed_body(groups, queries, keys, values, doc_ids, plan, w_out):
    parts = lax.axis_size("ctx")
    rows = queries.shape[0]
    heads = queries.shape[1] // HEAD_DIM
    width = w_out.shape[1]
    group, half = parts // groups, groups // 2
    bf16 = jnp.bfloat16
    params = pltpu.CompilerParams(vmem_limit_bytes=VMEM_LIMIT)
    pair = [(g, g ^ 1) for g in range(groups)]
    kv_rows = 2 * rows + META
    w_pair = lax.ppermute(w_out, "head", pair)
    block, q_block, kv_block = pl.pallas_call(
        functools.partial(pack_kernel, parts, heads),
        out_shape=[
            jax.ShapeDtypeStruct((heads * rows + kv_rows, HEAD_DIM), bf16),
            jax.ShapeDtypeStruct((heads * rows, HEAD_DIM), bf16),
            jax.ShapeDtypeStruct((kv_rows, HEAD_DIM), bf16),
        ],
        in_specs=[SMEM, VMEM, VMEM, VMEM, VMEM],
        out_specs=[VMEM] * 3,
        compiler_params=pltpu.CompilerParams(vmem_limit_bytes=PACK_LIMIT),
        name="pack",
    )(plan, queries, keys, values, doc_ids.reshape(1, rows))
    near, far_kv, far_q = spread_first(block, q_block, kv_block, parts)
    count = parts // 2
    arrived, halves = [], []
    last = parts - 1
    slot_groups = [range(count), range(count, count + 1), range(count + 1, last), range(last, parts)]
    for slots in slot_groups:
        inputs = [*near, *far_kv]
        if slots[0] >= count:
            inputs += far_q[slots[0] - count : slots[-1] + 1 - count]
        many = len(slots)
        out_rows = count * many * rows // parts
        send, keep = pl.pallas_call(
            functools.partial(attend_kernel, parts, heads, 1.0 / math.sqrt(HEAD_DIM), tuple(slots)),
            out_shape=[jax.ShapeDtypeStruct((out_rows, heads * HEAD_DIM), bf16)] * 2,
            in_specs=[ANY] * len(inputs),
            out_specs=[ANY, ANY],
            scratch_shapes=[
                pltpu.VMEM((many, heads * rows, HEAD_DIM), bf16),
                pltpu.VMEM((parts, kv_rows, HEAD_DIM), bf16),
                pltpu.VMEM((2, out_rows, heads * HEAD_DIM), bf16),
                pltpu.SMEM((2, parts), jnp.float32),
                pltpu.SemaphoreType.DMA((count + parts,)),
            ],
            compiler_params=params,
            name="attend",
        )(*inputs)
        if slots[0] == 0:
            send, far_q = lax.optimization_barrier((send, far_q))
            second = spread_second(far_q, parts)
            far_q = [far_q]
        if slots[0] == count:
            send, second = lax.optimization_barrier((send, second))
            far_q = spread_third(far_q[0], second, parts)
        halves += [keep, lax.ppermute(send, "head", pair)]
    sums = pl.pallas_call(
        functools.partial(project_kernel, group, half, parts, slot_groups),
        out_shape=[jax.ShapeDtypeStruct((rows, width), bf16)] * count,
        in_specs=[VMEM] * (2 * len(slot_groups) + 2),
        out_specs=[VMEM] * count,
        scratch_shapes=[
            pltpu.VMEM((count * rows, heads * HEAD_DIM), bf16),
            pltpu.VMEM((count * rows, heads * HEAD_DIM), bf16),
            pltpu.VMEM((count * rows, width), jnp.float32),
        ],
        compiler_params=params,
        name="project",
    )(*halves, w_out, w_pair)
    for k in range(count):
        pairs = []
        for c in range(parts):
            for g in range(groups):
                high = ((c % group) * half + g // 2) ^ k
                pairs.append((c * groups + g, (high * 2 + g % 2) * groups + c // group))
        arrived.append(lax.ppermute(sums[k], ("ctx", "head"), pairs))
    return pl.pallas_call(
        functools.partial(final_kernel, group, half),
        out_shape=jax.ShapeDtypeStruct((rows, group * width), bf16),
        in_specs=[VMEM] * count,
        out_specs=VMEM,
        compiler_params=params,
        name="final_sum",
    )(*arrived)


def spread_rows(block, order, parts):
    shaped = block.reshape(parts, block.shape[0] // parts, block.shape[1])
    return jnp.take(shaped, order, axis=0).reshape(block.shape)


def attend(query_rows, row_pos, row_start, all_keys, all_values):
    n_rows = query_rows.shape[0]
    kv_local = all_keys.shape[1] // HEAD_DIM
    group_size = query_rows.shape[1] // all_keys.shape[1]
    q_heads = query_rows.reshape(n_rows, kv_local, group_size, HEAD_DIM).transpose(1, 0, 2, 3)
    q_heads = q_heads.reshape(kv_local, n_rows * group_size, HEAD_DIM)
    pos_rows = jnp.repeat(row_pos, group_size)
    start_rows = jnp.repeat(row_start, group_size)
    q_block = min(n_rows, max(1, 512 // group_size))
    block_rows = q_block * group_size
    n_qblocks = n_rows // q_block
    score_scale = 1.0 / math.sqrt(HEAD_DIM)
    total_keys = all_keys.shape[0]
    key_size = math.gcd(total_keys, 512)
    n_kblocks = total_keys // key_size
    key_tiles = all_keys.reshape(n_kblocks, key_size, kv_local, HEAD_DIM)
    value_tiles = all_values.reshape(n_kblocks, key_size, kv_local, HEAD_DIM)
    initial = (
        jnp.full((kv_local, n_rows * group_size), NEG_FILL, jnp.float32),
        jnp.zeros((kv_local, n_rows * group_size), jnp.float32),
        jnp.zeros((kv_local, n_rows * group_size, HEAD_DIM), jnp.float32),
    )

    def one_query_block(block_index, state):
        run_max, run_sum, run_acc = state
        offset = block_index * block_rows
        q_part = lax.dynamic_slice_in_dim(q_heads, offset, block_rows, 1)
        pos_part = lax.dynamic_slice_in_dim(pos_rows, offset, block_rows, 0)
        start_part = lax.dynamic_slice_in_dim(start_rows, offset, block_rows, 0)
        first_block = jnp.clip(jnp.min(start_part) // key_size, 0, n_kblocks)
        last_block = jnp.clip(jnp.max(pos_part) // key_size + 1, 0, n_kblocks)

        def add_tile(key_index, inner):
            block_max, block_sum, block_acc = inner
            key_tile = lax.dynamic_index_in_dim(key_tiles, key_index, 0, keepdims=False)
            value_tile = lax.dynamic_index_in_dim(value_tiles, key_index, 0, keepdims=False)
            scores = (
                jnp.einsum("grd,kgd->grk", q_part, key_tile, preferred_element_type=jnp.float32)
                * score_scale
            )
            key_pos = key_index * key_size + jnp.arange(key_size, dtype=jnp.int32)
            allowed = (key_pos[None, :] >= start_part[:, None]) & (
                key_pos[None, :] <= pos_part[:, None]
            )
            scores = jnp.where(allowed[None], scores, NEG_FILL)
            new_max = jnp.maximum(block_max, jnp.max(scores, axis=-1))
            expo = jnp.where(allowed[None], jnp.exp(scores - new_max[..., None]), 0.0)
            rescale = jnp.exp(block_max - new_max)
            block_sum = block_sum * rescale + jnp.sum(expo, axis=-1)
            block_acc = block_acc * rescale[..., None] + jnp.einsum(
                "grk,kgd->grd",
                expo.astype(jnp.bfloat16),
                value_tile,
                preferred_element_type=jnp.float32,
            )
            return (new_max, block_sum, block_acc)

        def one_key_block(key_index, inner):
            tile_low = key_index * key_size
            tile_high = tile_low + key_size - 1
            meets = jnp.any((start_part <= tile_high) & (pos_part >= tile_low))
            return lax.cond(
                meets, lambda carried: add_tile(key_index, carried), lambda carried: carried, inner
            )

        inner = (
            lax.dynamic_slice_in_dim(run_max, offset, block_rows, 1),
            lax.dynamic_slice_in_dim(run_sum, offset, block_rows, 1),
            lax.dynamic_slice_in_dim(run_acc, offset, block_rows, 1),
        )
        new_max, new_sum, new_acc = lax.fori_loop(first_block, last_block, one_key_block, inner)
        run_max = lax.dynamic_update_slice_in_dim(run_max, new_max, offset, 1)
        run_sum = lax.dynamic_update_slice_in_dim(run_sum, new_sum, offset, 1)
        run_acc = lax.dynamic_update_slice_in_dim(run_acc, new_acc, offset, 1)
        return (run_max, run_sum, run_acc)

    final_max, final_sum, final_acc = lax.fori_loop(0, n_qblocks, one_query_block, initial)
    result = final_acc / final_sum[..., None]
    result = result.reshape(kv_local, n_rows, group_size, HEAD_DIM).transpose(1, 0, 2, 3)
    return result.reshape(n_rows, kv_local * group_size * HEAD_DIM).astype(jnp.bfloat16)


def body(queries, keys, values, doc_ids, plan, w_out):
    n_rows = queries.shape[0]
    parts = lax.axis_size("ctx")
    my_index = lax.axis_index("ctx")
    all_ids, all_plan = (
        lax.all_gather(doc_ids, "ctx", axis=0, tiled=True),
        lax.all_gather(plan, "ctx", axis=0, tiled=True),
    )
    all_keys, all_values = (
        lax.all_gather(keys, "ctx", axis=0, tiled=True),
        lax.all_gather(values, "ctx", axis=0, tiled=True),
    )
    doc_range = jnp.arange(DOCS, dtype=jnp.int32)
    doc_first = jnp.sum((all_ids[None, :] < doc_range[:, None]).astype(jnp.int32), axis=1)
    local_pos = my_index * n_rows + jnp.arange(n_rows, dtype=jnp.int32)
    ids_here = jnp.take(all_ids, local_pos)
    local_out = attend(
        queries,
        local_pos,
        jnp.sum(jnp.where(ids_here[:, None] == doc_range[None, :], doc_first[None, :], 0), axis=1),
        all_keys,
        all_values,
    )
    attended = lax.all_to_all(
        spread_rows(local_out, plan[0], parts), "ctx", split_axis=0, concat_axis=0, tiled=True
    )
    stacked = jnp.dot(
        lax.all_gather(attended, "ctx", axis=0, tiled=True),
        w_out,
        preferred_element_type=jnp.float32,
    )
    partial_sum = lax.all_to_all(
        stacked.astype(jnp.bfloat16), "ctx", split_axis=0, concat_axis=1, tiled=True
    ).astype(stacked.dtype)
    summed = lax.psum_scatter(
        partial_sum.astype(jnp.bfloat16), "head", scatter_dimension=1, tiled=True
    )
    return summed


def fits(parts, groups, rows, width):
    powers = all(n & (n - 1) == 0 for n in (parts, groups))
    window = parts * rows * width * 2
    whole = rows % (16 * parts) == 0 and groups % 2 == 0 and parts % groups == 0
    return powers and whole and 8 * window <= VMEM_LIMIT


def solution(mesh):
    parts, groups = mesh.shape["ctx"], mesh.shape["head"]

    def one_device(queries, keys, values, doc_ids, plan, w_out):
        one_pair = keys.shape[1] == HEAD_DIM
        if one_pair and fits(parts, groups, queries.shape[0], queries.shape[1]):
            return packed_body(groups, queries, keys, values, doc_ids, plan, w_out)
        return body(queries, keys, values, doc_ids, plan, w_out)

    return jax.shard_map(
        one_device,
        mesh=mesh,
        in_specs=(
            P("ctx", "head"),
            P("ctx", "head"),
            P("ctx", "head"),
            P("ctx"),
            P("ctx", None),
            P("head", "ctx"),
        ),
        out_specs=P("ctx", "head"),
        check_vma=False,
    )
```

```python
import functools
import math

import jax
import jax.numpy as jnp
from jax import lax
from jax.experimental import pallas as pl
from jax.experimental.pallas import tpu as pltpu
from jax.sharding import PartitionSpec as P

HEAD_DIM = 128
DOCS = 16
META = 16
NEG_FILL = -1e30
VMEM_LIMIT = 24 * 1024 * 1024
PACK_LIMIT = 56 * 1024 * 1024

ANY = pl.BlockSpec(memory_space=pl.ANY)
VMEM = pl.BlockSpec(memory_space=pltpu.VMEM)
SMEM = pl.BlockSpec(memory_space=pltpu.SMEM)


def pack_kernel(parts, heads, plan_ref, q_ref, k_ref, v_ref, ids_ref, all_out, q_out, kv_out):
    rows = q_ref.shape[0]
    piece = rows // parts
    lane = lax.broadcasted_iota(jnp.int32, (1, rows), 1)
    source = jnp.zeros((1, rows), jnp.int32)
    for j in range(parts):
        p = plan_ref[0, j]
        for h in range(heads):
            moved = q_ref[
                pl.ds(pl.multiple_of(p * piece, piece), piece), h * HEAD_DIM : (h + 1) * HEAD_DIM
            ]
            q_out[h * rows + j * piece : h * rows + (j + 1) * piece, :] = moved
            all_out[h * rows + j * piece : h * rows + (j + 1) * piece, :] = moved
        source = jnp.where(
            (lane >= j * piece) & (lane < (j + 1) * piece), (p - j) * piece + lane, source
        )
    ids = ids_ref[...].astype(jnp.float32)
    row = lax.broadcasted_iota(jnp.int32, (META, rows), 0)
    from_row = lax.broadcasted_iota(jnp.int32, (rows, rows), 0)
    chosen = (from_row == source).astype(jnp.float32)
    ids_rows = jnp.broadcast_to(ids, (META, rows))
    ids_moved = jnp.dot(ids_rows, chosen, preferred_element_type=jnp.float32)
    positions = jnp.broadcast_to(source.astype(jnp.float32), (META, rows))
    meta = jnp.where(row == 0, ids_rows, jnp.where(row == 1, ids_moved, positions))
    for out_ref, base in ((all_out, heads * rows), (kv_out, 0)):
        out_ref[base : base + rows, :] = k_ref[...]
        out_ref[base + rows : base + 2 * rows, :] = v_ref[...]
        out_ref[base + 2 * rows :, :] = meta.astype(jnp.bfloat16)


def attend_kernel(parts, heads, scale, slots, *refs):
    half, many = parts // 2, len(slots)
    near, far, refs = refs[:half], refs[half : 2 * half], refs[2 * half :]
    q_blocks = [near[k] for k in slots if k < half]
    if not q_blocks:
        q_blocks, refs = refs[:many], refs[many:]
    send_ref, keep_ref, q_held, kv_held, rows_ref, ends, sems = refs
    rows = q_held.shape[1] // heads
    piece = rows // parts
    me = lax.axis_index("ctx")
    other = 1 - lax.rem(lax.axis_index("head"), 2)
    q_rows = heads * rows
    copies = [
        pltpu.make_async_copy(
            near[k].at[q_rows:], kv_held.at[jnp.bitwise_xor(me, k)], sems.at[half + k]
        )
        for k in range(half)
    ] + [
        pltpu.make_async_copy(
            far[k], kv_held.at[jnp.bitwise_xor(me, half + k)], sems.at[2 * half + k]
        )
        for k in range(half)
    ] + [
        pltpu.make_async_copy(q_blocks[i].at[:q_rows], q_held.at[i], sems.at[i])
        for i in range(many)
    ]
    for copy in copies:
        copy.start()
    for copy in copies:
        copy.wait()

    def ids_of(block):
        return kv_held[block, 2 * rows :, :].astype(jnp.float32)

    for b in range(parts):
        ids = ids_of(b)[0:1]
        ends[0, b] = jnp.min(ids)
        ends[1, b] = jnp.max(ids)

    def one_block(i, carry):
        d = jnp.bitwise_xor(me, slots[0] + i)
        turned = ids_of(d).T
        q_ids, q_pos = turned[:, 1:2], turned[:, 2:3]
        start = jnp.int32(0)
        for b in range(parts):
            start = start + (ends[1, b] < ends[0, d]).astype(jnp.int32)
        b0 = lax.div(start, 2) * 2
        tiles = lax.div(d, 2) + 1 - lax.div(start, 2)
        for w in range(1, half + 1):

            @pl.when(tiles == w)
            def _(w=w):
                span = 2 * w * rows
                k_ids = jnp.concatenate([ids_of(b0 + n)[0:1] for n in range(2 * w)], axis=1)
                k_pos = lax.broadcasted_iota(jnp.int32, (1, span), 1) + (b0 - d) * rows
                allowed = (k_ids == q_ids) & (k_pos.astype(jnp.float32) <= q_pos)
                bias = jnp.where(allowed, 0.0, NEG_FILL)
                keys = kv_held[pl.ds(b0, 2 * w), :rows, :].reshape(span, HEAD_DIM)
                vals = kv_held[pl.ds(b0, 2 * w), rows : 2 * rows, :].reshape(span, HEAD_DIM)
                vals = jnp.concatenate([vals, jnp.ones((span, HEAD_DIM), jnp.bfloat16)], axis=1)
                for h in range(heads):
                    q = q_held[i, h * rows : (h + 1) * rows, :]
                    s = lax.dot_general(
                        q, keys, (((1,), (1,)), ((), ())), preferred_element_type=jnp.float32
                    )
                    s = s + bias
                    top = jnp.max(s, axis=1, keepdims=True)
                    e = jnp.exp2((s - top) * (scale * math.log2(math.e)))
                    o = jnp.dot(e.astype(jnp.bfloat16), vals, preferred_element_type=jnp.float32)
                    o = (o[:, :HEAD_DIM] / o[:, HEAD_DIM:]).astype(jnp.bfloat16)
                    for j in range(parts):
                        at = pl.multiple_of((j // 2) * many * piece + i * piece, piece)
                        rows_ref[
                            jnp.bitwise_xor(other, j % 2),
                            pl.ds(at, piece),
                            h * HEAD_DIM : (h + 1) * HEAD_DIM,
                        ] = o[j * piece : (j + 1) * piece, :]

        return carry

    lax.fori_loop(0, many, one_block, 0)
    out = [
        pltpu.make_async_copy(rows_ref.at[0], send_ref, sems.at[0]),
        pltpu.make_async_copy(rows_ref.at[1], keep_ref, sems.at[1]),
    ]
    for copy in out:
        copy.start()
    for copy in out:
        copy.wait()


def turn_of(plane, count):
    return (1 - (plane ^ (plane >> 1)) % 2) * (count - 1)


def project_kernel(group, half, parts, groups_of_slots, *refs):
    halves, refs = refs[: 2 * len(groups_of_slots)], refs[2 * len(groups_of_slots) :]
    w_ref, w_pair_ref, refs = refs[0], refs[1], refs[2:]
    out_refs, (x_keep, x_got, total) = refs[:-3], refs[-3:]
    count = len(out_refs)
    rows = out_refs[0].shape[0]
    piece = rows // parts
    me = lax.axis_index("ctx")
    for n, slots in enumerate(groups_of_slots):
        for held, part in ((x_keep, halves[2 * n]), (x_got, halves[2 * n + 1])):
            for i, slot in enumerate(slots):
                d = jnp.bitwise_xor(me, slot)
                for a in range(count):
                    at = pl.ds(pl.multiple_of(a * rows + d * piece, piece), piece)
                    first = (a * len(slots) + i) * piece
                    held[at, :] = part[first : first + piece, :]
    total[...] = jnp.dot(x_keep[...], w_ref[...], preferred_element_type=jnp.float32) + jnp.dot(
        x_got[...], w_pair_ref[...], preferred_element_type=jnp.float32
    )
    mine = lax.rem(me, group) * half + lax.div(lax.axis_index("head"), 2)
    mine = jnp.bitwise_xor(mine, turn_of(lax.div(me, group), count))
    for k, out_ref in enumerate(out_refs):
        at = pl.ds(pl.multiple_of(jnp.bitwise_xor(mine, k) * rows, rows), rows)
        out_ref[...] = total[at, :].astype(jnp.bfloat16)


def final_kernel(group, half, *refs):
    blocks, out_ref = refs[:-1], refs[-1]
    cols = blocks[0].shape[1]
    high = lax.div(lax.axis_index("ctx"), 2)
    high = jnp.bitwise_xor(high, turn_of(lax.axis_index("head"), len(blocks)))
    for first in range(0, len(blocks), half):
        part = lax.div(jnp.bitwise_xor(high, first), half)
        total = blocks[first][...].astype(jnp.float32)
        for k in range(first + 1, first + half):
            total = total + blocks[k][...].astype(jnp.float32)
        out_ref[:, pl.ds(pl.multiple_of(part * cols, cols), cols)] = total.astype(jnp.bfloat16)


def along_ctx(x, parts, k):
    return lax.ppermute(x, "ctx", [(i, i ^ k) for i in range(parts)])


def spread_first(block, q_block, kv_block, parts):
    half = parts // 2
    near, far_kv = {0: block}, {}
    far_kv[0] = along_ctx(kv_block, parts, half)
    far_kv[1] = along_ctx(kv_block, parts, half + 1)
    for k in [*range(2, half, 2), 1]:
        near[k] = along_ctx(block, parts, k)
    far_q = along_ctx(q_block, parts, half)
    near, far_kv = lax.optimization_barrier((near, far_kv))
    for k in range(2, half, 2):
        near[k + 1] = along_ctx(near[k], parts, 1)
        far_kv[k] = along_ctx(far_kv[0], parts, k)
        far_kv[k + 1] = along_ctx(far_kv[1], parts, k)
    return [near[k] for k in range(half)], [far_kv[k] for k in range(half)], far_q


def spread_second(far_q, parts):
    half = parts // 2
    got = {k: along_ctx(far_q, parts, k) for k in [*range(2, half, 2), 1]}
    return lax.optimization_barrier(got)


def spread_third(far_q, got, parts):
    half = parts // 2
    for k in range(2, half, 2):
        got[k + 1] = along_ctx(got[k], parts, 1)
    return [far_q] + [got[k] for k in range(1, half)]


def packed_body(groups, queries, keys, values, doc_ids, plan, w_out):
    parts = lax.axis_size("ctx")
    rows = queries.shape[0]
    heads = queries.shape[1] // HEAD_DIM
    width = w_out.shape[1]
    group, half = parts // groups, groups // 2
    bf16 = jnp.bfloat16
    params = pltpu.CompilerParams(vmem_limit_bytes=VMEM_LIMIT)
    pair = [(g, g ^ 1) for g in range(groups)]
    kv_rows = 2 * rows + META
    w_pair = lax.ppermute(w_out, "head", pair)
    block, q_block, kv_block = pl.pallas_call(
        functools.partial(pack_kernel, parts, heads),
        out_shape=[
            jax.ShapeDtypeStruct((heads * rows + kv_rows, HEAD_DIM), bf16),
            jax.ShapeDtypeStruct((heads * rows, HEAD_DIM), bf16),
            jax.ShapeDtypeStruct((kv_rows, HEAD_DIM), bf16),
        ],
        in_specs=[SMEM, VMEM, VMEM, VMEM, VMEM],
        out_specs=[VMEM] * 3,
        compiler_params=pltpu.CompilerParams(vmem_limit_bytes=PACK_LIMIT),
        name="pack",
    )(plan, queries, keys, values, doc_ids.reshape(1, rows))
    near, far_kv, far_q = spread_first(block, q_block, kv_block, parts)
    count = parts // 2
    arrived, halves = [], []
    last = parts - 1
    slot_groups = [range(count), range(count, count + 1), range(count + 1, last), range(last, parts)]
    for slots in slot_groups:
        inputs = [*near, *far_kv]
        if slots[0] >= count:
            inputs += far_q[slots[0] - count : slots[-1] + 1 - count]
        many = len(slots)
        out_rows = count * many * rows // parts
        send, keep = pl.pallas_call(
            functools.partial(attend_kernel, parts, heads, 1.0 / math.sqrt(HEAD_DIM), tuple(slots)),
            out_shape=[jax.ShapeDtypeStruct((out_rows, heads * HEAD_DIM), bf16)] * 2,
            in_specs=[ANY] * len(inputs),
            out_specs=[ANY, ANY],
            scratch_shapes=[
                pltpu.VMEM((many, heads * rows, HEAD_DIM), bf16),
                pltpu.VMEM((parts, kv_rows, HEAD_DIM), bf16),
                pltpu.VMEM((2, out_rows, heads * HEAD_DIM), bf16),
                pltpu.SMEM((2, parts), jnp.float32),
                pltpu.SemaphoreType.DMA((count + parts,)),
            ],
            compiler_params=params,
            name="attend",
        )(*inputs)
        if slots[0] == 0:
            send, far_q = lax.optimization_barrier((send, far_q))
            second = spread_second(far_q, parts)
            far_q = [far_q]
        if slots[0] == count:
            send, second = lax.optimization_barrier((send, second))
            far_q = spread_third(far_q[0], second, parts)
        halves += [keep, lax.ppermute(send, "head", pair)]
    sums = pl.pallas_call(
        functools.partial(project_kernel, group, half, parts, slot_groups),
        out_shape=[jax.ShapeDtypeStruct((rows, width), bf16)] * count,
        in_specs=[VMEM] * (2 * len(slot_groups) + 2),
        out_specs=[VMEM] * count,
        scratch_shapes=[
            pltpu.VMEM((count * rows, heads * HEAD_DIM), bf16),
            pltpu.VMEM((count * rows, heads * HEAD_DIM), bf16),
            pltpu.VMEM((count * rows, width), jnp.float32),
        ],
        compiler_params=params,
        name="project",
    )(*halves, w_out, w_pair)
    for k in range(count):
        pairs = []
        for c in range(parts):
            for g in range(groups):
                high = ((c % group) * half + g // 2) ^ k ^ turn_of(c // group, count)
                pairs.append((c * groups + g, (high * 2 + g % 2) * groups + c // group))
        arrived.append(lax.ppermute(sums[k], ("ctx", "head"), pairs))
    return pl.pallas_call(
        functools.partial(final_kernel, group, half),
        out_shape=jax.ShapeDtypeStruct((rows, group * width), bf16),
        in_specs=[VMEM] * count,
        out_specs=VMEM,
        compiler_params=params,
        name="final_sum",
    )(*arrived)


def spread_rows(block, order, parts):
    shaped = block.reshape(parts, block.shape[0] // parts, block.shape[1])
    return jnp.take(shaped, order, axis=0).reshape(block.shape)


def attend(query_rows, row_pos, row_start, all_keys, all_values):
    n_rows = query_rows.shape[0]
    kv_local = all_keys.shape[1] // HEAD_DIM
    group_size = query_rows.shape[1] // all_keys.shape[1]
    q_heads = query_rows.reshape(n_rows, kv_local, group_size, HEAD_DIM).transpose(1, 0, 2, 3)
    q_heads = q_heads.reshape(kv_local, n_rows * group_size, HEAD_DIM)
    pos_rows = jnp.repeat(row_pos, group_size)
    start_rows = jnp.repeat(row_start, group_size)
    q_block = min(n_rows, max(1, 512 // group_size))
    block_rows = q_block * group_size
    n_qblocks = n_rows // q_block
    score_scale = 1.0 / math.sqrt(HEAD_DIM)
    total_keys = all_keys.shape[0]
    key_size = math.gcd(total_keys, 512)
    n_kblocks = total_keys // key_size
    key_tiles = all_keys.reshape(n_kblocks, key_size, kv_local, HEAD_DIM)
    value_tiles = all_values.reshape(n_kblocks, key_size, kv_local, HEAD_DIM)
    initial = (
        jnp.full((kv_local, n_rows * group_size), NEG_FILL, jnp.float32),
        jnp.zeros((kv_local, n_rows * group_size), jnp.float32),
        jnp.zeros((kv_local, n_rows * group_size, HEAD_DIM), jnp.float32),
    )

    def one_query_block(block_index, state):
        run_max, run_sum, run_acc = state
        offset = block_index * block_rows
        q_part = lax.dynamic_slice_in_dim(q_heads, offset, block_rows, 1)
        pos_part = lax.dynamic_slice_in_dim(pos_rows, offset, block_rows, 0)
        start_part = lax.dynamic_slice_in_dim(start_rows, offset, block_rows, 0)
        first_block = jnp.clip(jnp.min(start_part) // key_size, 0, n_kblocks)
        last_block = jnp.clip(jnp.max(pos_part) // key_size + 1, 0, n_kblocks)

        def add_tile(key_index, inner):
            block_max, block_sum, block_acc = inner
            key_tile = lax.dynamic_index_in_dim(key_tiles, key_index, 0, keepdims=False)
            value_tile = lax.dynamic_index_in_dim(value_tiles, key_index, 0, keepdims=False)
            scores = (
                jnp.einsum("grd,kgd->grk", q_part, key_tile, preferred_element_type=jnp.float32)
                * score_scale
            )
            key_pos = key_index * key_size + jnp.arange(key_size, dtype=jnp.int32)
            allowed = (key_pos[None, :] >= start_part[:, None]) & (
                key_pos[None, :] <= pos_part[:, None]
            )
            scores = jnp.where(allowed[None], scores, NEG_FILL)
            new_max = jnp.maximum(block_max, jnp.max(scores, axis=-1))
            expo = jnp.where(allowed[None], jnp.exp(scores - new_max[..., None]), 0.0)
            rescale = jnp.exp(block_max - new_max)
            block_sum = block_sum * rescale + jnp.sum(expo, axis=-1)
            block_acc = block_acc * rescale[..., None] + jnp.einsum(
                "grk,kgd->grd",
                expo.astype(jnp.bfloat16),
                value_tile,
                preferred_element_type=jnp.float32,
            )
            return (new_max, block_sum, block_acc)

        def one_key_block(key_index, inner):
            tile_low = key_index * key_size
            tile_high = tile_low + key_size - 1
            meets = jnp.any((start_part <= tile_high) & (pos_part >= tile_low))
            return lax.cond(
                meets, lambda carried: add_tile(key_index, carried), lambda carried: carried, inner
            )

        inner = (
            lax.dynamic_slice_in_dim(run_max, offset, block_rows, 1),
            lax.dynamic_slice_in_dim(run_sum, offset, block_rows, 1),
            lax.dynamic_slice_in_dim(run_acc, offset, block_rows, 1),
        )
        new_max, new_sum, new_acc = lax.fori_loop(first_block, last_block, one_key_block, inner)
        run_max = lax.dynamic_update_slice_in_dim(run_max, new_max, offset, 1)
        run_sum = lax.dynamic_update_slice_in_dim(run_sum, new_sum, offset, 1)
        run_acc = lax.dynamic_update_slice_in_dim(run_acc, new_acc, offset, 1)
        return (run_max, run_sum, run_acc)

    final_max, final_sum, final_acc = lax.fori_loop(0, n_qblocks, one_query_block, initial)
    result = final_acc / final_sum[..., None]
    result = result.reshape(kv_local, n_rows, group_size, HEAD_DIM).transpose(1, 0, 2, 3)
    return result.reshape(n_rows, kv_local * group_size * HEAD_DIM).astype(jnp.bfloat16)


def body(queries, keys, values, doc_ids, plan, w_out):
    n_rows = queries.shape[0]
    parts = lax.axis_size("ctx")
    my_index = lax.axis_index("ctx")
    all_ids, all_plan = (
        lax.all_gather(doc_ids, "ctx", axis=0, tiled=True),
        lax.all_gather(plan, "ctx", axis=0, tiled=True),
    )
    all_keys, all_values = (
        lax.all_gather(keys, "ctx", axis=0, tiled=True),
        lax.all_gather(values, "ctx", axis=0, tiled=True),
    )
    doc_range = jnp.arange(DOCS, dtype=jnp.int32)
    doc_first = jnp.sum((all_ids[None, :] < doc_range[:, None]).astype(jnp.int32), axis=1)
    local_pos = my_index * n_rows + jnp.arange(n_rows, dtype=jnp.int32)
    ids_here = jnp.take(all_ids, local_pos)
    local_out = attend(
        queries,
        local_pos,
        jnp.sum(jnp.where(ids_here[:, None] == doc_range[None, :], doc_first[None, :], 0), axis=1),
        all_keys,
        all_values,
    )
    attended = lax.all_to_all(
        spread_rows(local_out, plan[0], parts), "ctx", split_axis=0, concat_axis=0, tiled=True
    )
    stacked = jnp.dot(
        lax.all_gather(attended, "ctx", axis=0, tiled=True),
        w_out,
        preferred_element_type=jnp.float32,
    )
    partial_sum = lax.all_to_all(
        stacked.astype(jnp.bfloat16), "ctx", split_axis=0, concat_axis=1, tiled=True
    ).astype(stacked.dtype)
    summed = lax.psum_scatter(
        partial_sum.astype(jnp.bfloat16), "head", scatter_dimension=1, tiled=True
    )
    return summed


def fits(parts, groups, rows, width):
    powers = all(n & (n - 1) == 0 for n in (parts, groups))
    window = parts * rows * width * 2
    whole = rows % (16 * parts) == 0 and groups % 2 == 0 and parts % groups == 0
    return powers and whole and 8 * window <= VMEM_LIMIT


def solution(mesh):
    parts, groups = mesh.shape["ctx"], mesh.shape["head"]

    def one_device(queries, keys, values, doc_ids, plan, w_out):
        one_pair = keys.shape[1] == HEAD_DIM
        if one_pair and fits(parts, groups, queries.shape[0], queries.shape[1]):
            return packed_body(groups, queries, keys, values, doc_ids, plan, w_out)
        return body(queries, keys, values, doc_ids, plan, w_out)

    return jax.shard_map(
        one_device,
        mesh=mesh,
        in_specs=(
            P("ctx", "head"),
            P("ctx", "head"),
            P("ctx", "head"),
            P("ctx"),
            P("ctx", None),
            P("head", "ctx"),
        ),
        out_specs=P("ctx", "head"),
        check_vma=False,
    )
```

```python
import functools
import math

import jax
import jax.numpy as jnp
from jax import lax
from jax.experimental import pallas as pl
from jax.experimental.pallas import tpu as pltpu
from jax.sharding import PartitionSpec as P

HEAD_DIM = 128
DOCS = 16
META = 16
NEG_FILL = -1e30
VMEM_LIMIT = 24 * 1024 * 1024
PACK_LIMIT = 56 * 1024 * 1024

ANY = pl.BlockSpec(memory_space=pl.ANY)
VMEM = pl.BlockSpec(memory_space=pltpu.VMEM)
SMEM = pl.BlockSpec(memory_space=pltpu.SMEM)


def pack_kernel(parts, heads, plan_ref, q_ref, k_ref, v_ref, ids_ref, all_out, q_out, kv_out):
    rows = q_ref.shape[0]
    piece = rows // parts
    lane = lax.broadcasted_iota(jnp.int32, (1, rows), 1)
    source = jnp.zeros((1, rows), jnp.int32)
    for j in range(parts):
        p = plan_ref[0, j]
        for h in range(heads):
            moved = q_ref[
                pl.ds(pl.multiple_of(p * piece, piece), piece), h * HEAD_DIM : (h + 1) * HEAD_DIM
            ]
            q_out[h * rows + j * piece : h * rows + (j + 1) * piece, :] = moved
            all_out[h * rows + j * piece : h * rows + (j + 1) * piece, :] = moved
        source = jnp.where(
            (lane >= j * piece) & (lane < (j + 1) * piece), (p - j) * piece + lane, source
        )
    ids = ids_ref[...].astype(jnp.float32)
    row = lax.broadcasted_iota(jnp.int32, (META, rows), 0)
    from_row = lax.broadcasted_iota(jnp.int32, (rows, rows), 0)
    chosen = (from_row == source).astype(jnp.float32)
    ids_rows = jnp.broadcast_to(ids, (META, rows))
    ids_moved = jnp.dot(ids_rows, chosen, preferred_element_type=jnp.float32)
    positions = jnp.broadcast_to(source.astype(jnp.float32), (META, rows))
    meta = jnp.where(row == 0, ids_rows, jnp.where(row == 1, ids_moved, positions))
    for out_ref, base in ((all_out, heads * rows), (kv_out, 0)):
        out_ref[base : base + rows, :] = k_ref[...]
        out_ref[base + rows : base + 2 * rows, :] = v_ref[...]
        out_ref[base + 2 * rows :, :] = meta.astype(jnp.bfloat16)


def attend_kernel(parts, heads, scale, slots, *refs):
    half, many = parts // 2, len(slots)
    near, far, refs = refs[:half], refs[half : 2 * half], refs[2 * half :]
    q_blocks = [near[k] for k in slots if k < half]
    if not q_blocks:
        q_blocks, refs = refs[:many], refs[many:]
    send_ref, keep_ref, q_held, kv_held, rows_ref, ends = refs
    rows = q_held.shape[1] // heads
    piece = rows // parts
    me = lax.axis_index("ctx")
    other = 1 - lax.rem(lax.axis_index("head"), 2)
    q_rows = heads * rows
    for k in range(half):
        kv_held[jnp.bitwise_xor(me, k)] = near[k][q_rows:, :]
        kv_held[jnp.bitwise_xor(me, half + k)] = far[k][...]
    for i in range(many):
        q_held[i] = q_blocks[i][:q_rows, :]

    def ids_of(block):
        return kv_held[block, 2 * rows :, :].astype(jnp.float32)

    for b in range(parts):
        ids = ids_of(b)[0:1]
        ends[0, b] = jnp.min(ids)
        ends[1, b] = jnp.max(ids)

    def one_block(i, carry):
        d = jnp.bitwise_xor(me, slots[0] + i)
        turned = ids_of(d).T
        q_ids, q_pos = turned[:, 1:2], turned[:, 2:3]
        start = jnp.int32(0)
        for b in range(parts):
            start = start + (ends[1, b] < ends[0, d]).astype(jnp.int32)
        b0 = lax.div(start, 2) * 2
        tiles = lax.div(d, 2) + 1 - lax.div(start, 2)
        for w in range(1, half + 1):

            @pl.when(tiles == w)
            def _(w=w):
                span = 2 * w * rows
                k_ids = jnp.concatenate([ids_of(b0 + n)[0:1] for n in range(2 * w)], axis=1)
                k_pos = lax.broadcasted_iota(jnp.int32, (1, span), 1) + (b0 - d) * rows
                allowed = (k_ids == q_ids) & (k_pos.astype(jnp.float32) <= q_pos)
                bias = jnp.where(allowed, 0.0, NEG_FILL)
                keys = kv_held[pl.ds(b0, 2 * w), :rows, :].reshape(span, HEAD_DIM)
                vals = kv_held[pl.ds(b0, 2 * w), rows : 2 * rows, :].reshape(span, HEAD_DIM)
                vals = jnp.concatenate([vals, jnp.ones((span, HEAD_DIM), jnp.bfloat16)], axis=1)
                for h in range(heads):
                    q = q_held[i, h * rows : (h + 1) * rows, :]
                    s = lax.dot_general(
                        q, keys, (((1,), (1,)), ((), ())), preferred_element_type=jnp.float32
                    )
                    s = s + bias
                    top = jnp.max(s, axis=1, keepdims=True)
                    e = jnp.exp2((s - top) * (scale * math.log2(math.e)))
                    o = jnp.dot(e.astype(jnp.bfloat16), vals, preferred_element_type=jnp.float32)
                    o = (o[:, :HEAD_DIM] / o[:, HEAD_DIM:]).astype(jnp.bfloat16)
                    for j in range(parts):
                        at = pl.multiple_of((j // 2) * many * piece + i * piece, piece)
                        rows_ref[
                            jnp.bitwise_xor(other, j % 2),
                            pl.ds(at, piece),
                            h * HEAD_DIM : (h + 1) * HEAD_DIM,
                        ] = o[j * piece : (j + 1) * piece, :]

        return carry

    lax.fori_loop(0, many, one_block, 0)
    send_ref[...] = rows_ref[0]
    keep_ref[...] = rows_ref[1]


def turn_of(plane, count):
    return (1 - (plane ^ (plane >> 1)) % 2) * (count - 1)


def project_kernel(group, half, parts, groups_of_slots, *refs):
    halves, refs = refs[: 2 * len(groups_of_slots)], refs[2 * len(groups_of_slots) :]
    w_ref, w_pair_ref, refs = refs[0], refs[1], refs[2:]
    out_refs, (x_keep, x_got, total) = refs[:-3], refs[-3:]
    count = len(out_refs)
    rows = out_refs[0].shape[0]
    piece = rows // parts
    me = lax.axis_index("ctx")
    for n, slots in enumerate(groups_of_slots):
        for held, part in ((x_keep, halves[2 * n]), (x_got, halves[2 * n + 1])):
            for i, slot in enumerate(slots):
                d = jnp.bitwise_xor(me, slot)
                for a in range(count):
                    at = pl.ds(pl.multiple_of(a * rows + d * piece, piece), piece)
                    first = (a * len(slots) + i) * piece
                    held[at, :] = part[first : first + piece, :]
    total[...] = jnp.dot(x_keep[...], w_ref[...], preferred_element_type=jnp.float32) + jnp.dot(
        x_got[...], w_pair_ref[...], preferred_element_type=jnp.float32
    )
    mine = lax.rem(me, group) * half + lax.div(lax.axis_index("head"), 2)
    mine = jnp.bitwise_xor(mine, turn_of(lax.div(me, group), count))
    for k, out_ref in enumerate(out_refs):
        at = pl.ds(pl.multiple_of(jnp.bitwise_xor(mine, k) * rows, rows), rows)
        out_ref[...] = total[at, :].astype(jnp.bfloat16)


def final_kernel(group, half, *refs):
    blocks, out_ref = refs[:-1], refs[-1]
    cols = blocks[0].shape[1]
    high = lax.div(lax.axis_index("ctx"), 2)
    high = jnp.bitwise_xor(high, turn_of(lax.axis_index("head"), len(blocks)))
    for first in range(0, len(blocks), half):
        part = lax.div(jnp.bitwise_xor(high, first), half)
        total = blocks[first][...].astype(jnp.float32)
        for k in range(first + 1, first + half):
            total = total + blocks[k][...].astype(jnp.float32)
        out_ref[:, pl.ds(pl.multiple_of(part * cols, cols), cols)] = total.astype(jnp.bfloat16)


def along_ctx(x, parts, k):
    return lax.ppermute(x, "ctx", [(i, i ^ k) for i in range(parts)])


def spread_first(block, q_block, kv_block, parts):
    half = parts // 2
    near, far_kv = {0: block}, {}
    far_kv[0] = along_ctx(kv_block, parts, half)
    far_kv[1] = along_ctx(kv_block, parts, half + 1)
    for k in [*range(2, half, 2), 1]:
        near[k] = along_ctx(block, parts, k)
    far_q = along_ctx(q_block, parts, half)
    near, far_kv = lax.optimization_barrier((near, far_kv))
    for k in range(2, half, 2):
        near[k + 1] = along_ctx(near[k], parts, 1)
        far_kv[k] = along_ctx(far_kv[0], parts, k)
        far_kv[k + 1] = along_ctx(far_kv[1], parts, k)
    return [near[k] for k in range(half)], [far_kv[k] for k in range(half)], far_q


def spread_second(far_q, parts):
    half = parts // 2
    got = {k: along_ctx(far_q, parts, k) for k in [*range(2, half, 2), 1]}
    return lax.optimization_barrier(got)


def spread_third(far_q, got, parts):
    half = parts // 2
    for k in range(2, half, 2):
        got[k + 1] = along_ctx(got[k], parts, 1)
    return [far_q] + [got[k] for k in range(1, half)]


def packed_body(groups, queries, keys, values, doc_ids, plan, w_out):
    parts = lax.axis_size("ctx")
    rows = queries.shape[0]
    heads = queries.shape[1] // HEAD_DIM
    width = w_out.shape[1]
    group, half = parts // groups, groups // 2
    bf16 = jnp.bfloat16
    params = pltpu.CompilerParams(vmem_limit_bytes=VMEM_LIMIT)
    pair = [(g, g ^ 1) for g in range(groups)]
    kv_rows = 2 * rows + META
    w_pair = lax.ppermute(w_out, "head", pair)
    block, q_block, kv_block = pl.pallas_call(
        functools.partial(pack_kernel, parts, heads),
        out_shape=[
            jax.ShapeDtypeStruct((heads * rows + kv_rows, HEAD_DIM), bf16),
            jax.ShapeDtypeStruct((heads * rows, HEAD_DIM), bf16),
            jax.ShapeDtypeStruct((kv_rows, HEAD_DIM), bf16),
        ],
        in_specs=[SMEM, VMEM, VMEM, VMEM, VMEM],
        out_specs=[VMEM] * 3,
        compiler_params=pltpu.CompilerParams(vmem_limit_bytes=PACK_LIMIT),
        name="pack",
    )(plan, queries, keys, values, doc_ids.reshape(1, rows))
    near, far_kv, far_q = spread_first(block, q_block, kv_block, parts)
    count = parts // 2
    arrived, halves = [], []
    last = parts - 1
    slot_groups = [range(count), range(count, count + 1), range(count + 1, last), range(last, parts)]
    for slots in slot_groups:
        inputs = [*near, *far_kv]
        if slots[0] >= count:
            inputs += far_q[slots[0] - count : slots[-1] + 1 - count]
        many = len(slots)
        out_rows = count * many * rows // parts
        send, keep = pl.pallas_call(
            functools.partial(attend_kernel, parts, heads, 1.0 / math.sqrt(HEAD_DIM), tuple(slots)),
            out_shape=[jax.ShapeDtypeStruct((out_rows, heads * HEAD_DIM), bf16)] * 2,
            in_specs=[VMEM] * len(inputs),
            out_specs=[VMEM, VMEM],
            scratch_shapes=[
                pltpu.VMEM((many, heads * rows, HEAD_DIM), bf16),
                pltpu.VMEM((parts, kv_rows, HEAD_DIM), bf16),
                pltpu.VMEM((2, out_rows, heads * HEAD_DIM), bf16),
                pltpu.SMEM((2, parts), jnp.float32),
            ],
            compiler_params=params,
            name="attend",
        )(*inputs)
        if slots[0] == 0:
            send, far_q = lax.optimization_barrier((send, far_q))
            second = spread_second(far_q, parts)
            far_q = [far_q]
        if slots[0] == count:
            send, second = lax.optimization_barrier((send, second))
            far_q = spread_third(far_q[0], second, parts)
        halves += [keep, lax.ppermute(send, "head", pair)]
    sums = pl.pallas_call(
        functools.partial(project_kernel, group, half, parts, slot_groups),
        out_shape=[jax.ShapeDtypeStruct((rows, width), bf16)] * count,
        in_specs=[VMEM] * (2 * len(slot_groups) + 2),
        out_specs=[VMEM] * count,
        scratch_shapes=[
            pltpu.VMEM((count * rows, heads * HEAD_DIM), bf16),
            pltpu.VMEM((count * rows, heads * HEAD_DIM), bf16),
            pltpu.VMEM((count * rows, width), jnp.float32),
        ],
        compiler_params=params,
        name="project",
    )(*halves, w_out, w_pair)
    for k in range(count):
        pairs = []
        for c in range(parts):
            for g in range(groups):
                high = ((c % group) * half + g // 2) ^ k ^ turn_of(c // group, count)
                pairs.append((c * groups + g, (high * 2 + g % 2) * groups + c // group))
        arrived.append(lax.ppermute(sums[k], ("ctx", "head"), pairs))
    return pl.pallas_call(
        functools.partial(final_kernel, group, half),
        out_shape=jax.ShapeDtypeStruct((rows, group * width), bf16),
        in_specs=[VMEM] * count,
        out_specs=VMEM,
        compiler_params=params,
        name="final_sum",
    )(*arrived)


def spread_rows(block, order, parts):
    shaped = block.reshape(parts, block.shape[0] // parts, block.shape[1])
    return jnp.take(shaped, order, axis=0).reshape(block.shape)


def attend(query_rows, row_pos, row_start, all_keys, all_values):
    n_rows = query_rows.shape[0]
    kv_local = all_keys.shape[1] // HEAD_DIM
    group_size = query_rows.shape[1] // all_keys.shape[1]
    q_heads = query_rows.reshape(n_rows, kv_local, group_size, HEAD_DIM).transpose(1, 0, 2, 3)
    q_heads = q_heads.reshape(kv_local, n_rows * group_size, HEAD_DIM)
    pos_rows = jnp.repeat(row_pos, group_size)
    start_rows = jnp.repeat(row_start, group_size)
    q_block = min(n_rows, max(1, 512 // group_size))
    block_rows = q_block * group_size
    n_qblocks = n_rows // q_block
    score_scale = 1.0 / math.sqrt(HEAD_DIM)
    total_keys = all_keys.shape[0]
    key_size = math.gcd(total_keys, 512)
    n_kblocks = total_keys // key_size
    key_tiles = all_keys.reshape(n_kblocks, key_size, kv_local, HEAD_DIM)
    value_tiles = all_values.reshape(n_kblocks, key_size, kv_local, HEAD_DIM)
    initial = (
        jnp.full((kv_local, n_rows * group_size), NEG_FILL, jnp.float32),
        jnp.zeros((kv_local, n_rows * group_size), jnp.float32),
        jnp.zeros((kv_local, n_rows * group_size, HEAD_DIM), jnp.float32),
    )

    def one_query_block(block_index, state):
        run_max, run_sum, run_acc = state
        offset = block_index * block_rows
        q_part = lax.dynamic_slice_in_dim(q_heads, offset, block_rows, 1)
        pos_part = lax.dynamic_slice_in_dim(pos_rows, offset, block_rows, 0)
        start_part = lax.dynamic_slice_in_dim(start_rows, offset, block_rows, 0)
        first_block = jnp.clip(jnp.min(start_part) // key_size, 0, n_kblocks)
        last_block = jnp.clip(jnp.max(pos_part) // key_size + 1, 0, n_kblocks)

        def add_tile(key_index, inner):
            block_max, block_sum, block_acc = inner
            key_tile = lax.dynamic_index_in_dim(key_tiles, key_index, 0, keepdims=False)
            value_tile = lax.dynamic_index_in_dim(value_tiles, key_index, 0, keepdims=False)
            scores = (
                jnp.einsum("grd,kgd->grk", q_part, key_tile, preferred_element_type=jnp.float32)
                * score_scale
            )
            key_pos = key_index * key_size + jnp.arange(key_size, dtype=jnp.int32)
            allowed = (key_pos[None, :] >= start_part[:, None]) & (
                key_pos[None, :] <= pos_part[:, None]
            )
            scores = jnp.where(allowed[None], scores, NEG_FILL)
            new_max = jnp.maximum(block_max, jnp.max(scores, axis=-1))
            expo = jnp.where(allowed[None], jnp.exp(scores - new_max[..., None]), 0.0)
            rescale = jnp.exp(block_max - new_max)
            block_sum = block_sum * rescale + jnp.sum(expo, axis=-1)
            block_acc = block_acc * rescale[..., None] + jnp.einsum(
                "grk,kgd->grd",
                expo.astype(jnp.bfloat16),
                value_tile,
                preferred_element_type=jnp.float32,
            )
            return (new_max, block_sum, block_acc)

        def one_key_block(key_index, inner):
            tile_low = key_index * key_size
            tile_high = tile_low + key_size - 1
            meets = jnp.any((start_part <= tile_high) & (pos_part >= tile_low))
            return lax.cond(
                meets, lambda carried: add_tile(key_index, carried), lambda carried: carried, inner
            )

        inner = (
            lax.dynamic_slice_in_dim(run_max, offset, block_rows, 1),
            lax.dynamic_slice_in_dim(run_sum, offset, block_rows, 1),
            lax.dynamic_slice_in_dim(run_acc, offset, block_rows, 1),
        )
        new_max, new_sum, new_acc = lax.fori_loop(first_block, last_block, one_key_block, inner)
        run_max = lax.dynamic_update_slice_in_dim(run_max, new_max, offset, 1)
        run_sum = lax.dynamic_update_slice_in_dim(run_sum, new_sum, offset, 1)
        run_acc = lax.dynamic_update_slice_in_dim(run_acc, new_acc, offset, 1)
        return (run_max, run_sum, run_acc)

    final_max, final_sum, final_acc = lax.fori_loop(0, n_qblocks, one_query_block, initial)
    result = final_acc / final_sum[..., None]
    result = result.reshape(kv_local, n_rows, group_size, HEAD_DIM).transpose(1, 0, 2, 3)
    return result.reshape(n_rows, kv_local * group_size * HEAD_DIM).astype(jnp.bfloat16)


def body(queries, keys, values, doc_ids, plan, w_out):
    n_rows = queries.shape[0]
    parts = lax.axis_size("ctx")
    my_index = lax.axis_index("ctx")
    all_ids, all_plan = (
        lax.all_gather(doc_ids, "ctx", axis=0, tiled=True),
        lax.all_gather(plan, "ctx", axis=0, tiled=True),
    )
    all_keys, all_values = (
        lax.all_gather(keys, "ctx", axis=0, tiled=True),
        lax.all_gather(values, "ctx", axis=0, tiled=True),
    )
    doc_range = jnp.arange(DOCS, dtype=jnp.int32)
    doc_first = jnp.sum((all_ids[None, :] < doc_range[:, None]).astype(jnp.int32), axis=1)
    local_pos = my_index * n_rows + jnp.arange(n_rows, dtype=jnp.int32)
    ids_here = jnp.take(all_ids, local_pos)
    local_out = attend(
        queries,
        local_pos,
        jnp.sum(jnp.where(ids_here[:, None] == doc_range[None, :], doc_first[None, :], 0), axis=1),
        all_keys,
        all_values,
    )
    attended = lax.all_to_all(
        spread_rows(local_out, plan[0], parts), "ctx", split_axis=0, concat_axis=0, tiled=True
    )
    stacked = jnp.dot(
        lax.all_gather(attended, "ctx", axis=0, tiled=True),
        w_out,
        preferred_element_type=jnp.float32,
    )
    partial_sum = lax.all_to_all(
        stacked.astype(jnp.bfloat16), "ctx", split_axis=0, concat_axis=1, tiled=True
    ).astype(stacked.dtype)
    summed = lax.psum_scatter(
        partial_sum.astype(jnp.bfloat16), "head", scatter_dimension=1, tiled=True
    )
    return summed


def fits(parts, groups, rows, width):
    powers = all(n & (n - 1) == 0 for n in (parts, groups))
    window = parts * rows * width * 2
    whole = rows % (16 * parts) == 0 and groups % 2 == 0 and parts % groups == 0
    return powers and whole and 8 * window <= VMEM_LIMIT


def solution(mesh):
    parts, groups = mesh.shape["ctx"], mesh.shape["head"]

    def one_device(queries, keys, values, doc_ids, plan, w_out):
        one_pair = keys.shape[1] == HEAD_DIM
        if one_pair and fits(parts, groups, queries.shape[0], queries.shape[1]):
            return packed_body(groups, queries, keys, values, doc_ids, plan, w_out)
        return body(queries, keys, values, doc_ids, plan, w_out)

    return jax.shard_map(
        one_device,
        mesh=mesh,
        in_specs=(
            P("ctx", "head"),
            P("ctx", "head"),
            P("ctx", "head"),
            P("ctx"),
            P("ctx", None),
            P("head", "ctx"),
        ),
        out_specs=P("ctx", "head"),
        check_vma=False,
    )
```

```python
import functools
import math

import jax
import jax.numpy as jnp
from jax import lax
from jax.experimental import pallas as pl
from jax.experimental.pallas import tpu as pltpu
from jax.sharding import PartitionSpec as P

HEAD_DIM = 128
DOCS = 16
META = 16
NEG_FILL = -1e30
VMEM_LIMIT = 24 * 1024 * 1024
PACK_LIMIT = 56 * 1024 * 1024

ANY = pl.BlockSpec(memory_space=pl.ANY)
VMEM = pl.BlockSpec(memory_space=pltpu.VMEM)
SMEM = pl.BlockSpec(memory_space=pltpu.SMEM)


def pack_kernel(parts, heads, plan_ref, q_ref, k_ref, v_ref, ids_ref, all_out, q_out, kv_out):
    rows = q_ref.shape[0]
    piece = rows // parts
    lane = lax.broadcasted_iota(jnp.int32, (1, rows), 1)
    source = jnp.zeros((1, rows), jnp.int32)
    for j in range(parts):
        p = plan_ref[0, j]
        for h in range(heads):
            moved = q_ref[
                pl.ds(pl.multiple_of(p * piece, piece), piece), h * HEAD_DIM : (h + 1) * HEAD_DIM
            ]
            q_out[h * rows + j * piece : h * rows + (j + 1) * piece, :] = moved
            all_out[h * rows + j * piece : h * rows + (j + 1) * piece, :] = moved
        source = jnp.where(
            (lane >= j * piece) & (lane < (j + 1) * piece), (p - j) * piece + lane, source
        )
    ids = ids_ref[...].astype(jnp.float32)
    row = lax.broadcasted_iota(jnp.int32, (META, rows), 0)
    from_row = lax.broadcasted_iota(jnp.int32, (rows, rows), 0)
    chosen = (from_row == source).astype(jnp.float32)
    ids_rows = jnp.broadcast_to(ids, (META, rows))
    ids_moved = jnp.dot(ids_rows, chosen, preferred_element_type=jnp.float32)
    positions = jnp.broadcast_to(source.astype(jnp.float32), (META, rows))
    meta = jnp.where(row == 0, ids_rows, jnp.where(row == 1, ids_moved, positions))
    for out_ref, base in ((all_out, heads * rows), (kv_out, 0)):
        out_ref[base : base + rows, :] = k_ref[...]
        out_ref[base + rows : base + 2 * rows, :] = v_ref[...]
        out_ref[base + 2 * rows :, :] = meta.astype(jnp.bfloat16)


def attend_kernel(parts, heads, scale, slots, *refs):
    half, many = parts // 2, len(slots)
    near, far, refs = refs[:half], refs[half : 2 * half], refs[2 * half :]
    q_blocks = [near[k] for k in slots if k < half]
    if not q_blocks:
        q_blocks, refs = refs[:many], refs[many:]
    send_ref, keep_ref, q_held, kv_held, rows_ref, ends = refs
    rows = q_held.shape[1] // heads
    piece = rows // parts
    me = lax.axis_index("ctx")
    other = 1 - lax.rem(lax.axis_index("head"), 2)
    q_rows = heads * rows
    for k in range(half):
        kv_held[jnp.bitwise_xor(me, k)] = near[k][q_rows:, :]
        kv_held[jnp.bitwise_xor(me, half + k)] = far[k][...]
    for i in range(many):
        q_held[i] = q_blocks[i][:q_rows, :]

    def ids_of(block):
        return kv_held[block, 2 * rows :, :].astype(jnp.float32)

    for b in range(parts):
        ids = ids_of(b)[0:1]
        ends[0, b] = jnp.min(ids)
        ends[1, b] = jnp.max(ids)

    def one_block(i, carry):
        d = jnp.bitwise_xor(me, slots[0] + i)
        turned = ids_of(d).T
        q_ids, q_pos = turned[:, 1:2], turned[:, 2:3]
        start = jnp.int32(0)
        for b in range(parts):
            start = start + (ends[1, b] < ends[0, d]).astype(jnp.int32)
        b0 = lax.div(start, 2) * 2
        tiles = lax.div(d, 2) + 1 - lax.div(start, 2)
        for w in range(1, half + 1):

            @pl.when(tiles == w)
            def _(w=w):
                span = 2 * w * rows
                k_ids = jnp.concatenate([ids_of(b0 + n)[0:1] for n in range(2 * w)], axis=1)
                k_pos = lax.broadcasted_iota(jnp.int32, (1, span), 1) + (b0 - d) * rows
                allowed = (k_ids == q_ids) & (k_pos.astype(jnp.float32) <= q_pos)
                bias = jnp.where(allowed, 0.0, NEG_FILL)
                keys = kv_held[pl.ds(b0, 2 * w), :rows, :].reshape(span, HEAD_DIM)
                vals = kv_held[pl.ds(b0, 2 * w), rows : 2 * rows, :].reshape(span, HEAD_DIM)
                vals = jnp.concatenate([vals, jnp.ones((span, HEAD_DIM), jnp.bfloat16)], axis=1)
                for h in range(heads):
                    q = q_held[i, h * rows : (h + 1) * rows, :]
                    s = lax.dot_general(
                        q, keys, (((1,), (1,)), ((), ())), preferred_element_type=jnp.float32
                    )
                    s = s + bias
                    top = jnp.max(s, axis=1, keepdims=True)
                    e = jnp.exp2((s - top) * (scale * math.log2(math.e)))
                    o = jnp.dot(e.astype(jnp.bfloat16), vals, preferred_element_type=jnp.float32)
                    o = (o[:, :HEAD_DIM] / o[:, HEAD_DIM:]).astype(jnp.bfloat16)
                    for j in range(parts):
                        at = pl.multiple_of((j // 2) * many * piece + i * piece, piece)
                        rows_ref[
                            jnp.bitwise_xor(other, j % 2),
                            pl.ds(at, piece),
                            h * HEAD_DIM : (h + 1) * HEAD_DIM,
                        ] = o[j * piece : (j + 1) * piece, :]

        return carry

    lax.fori_loop(0, many, one_block, 0)
    send_ref[...] = rows_ref[0]
    keep_ref[...] = rows_ref[1]


def turn_of(plane, count):
    return (1 - (plane ^ (plane >> 1)) % 2) * (count - 1)


def project_rows(slot_groups, halves, w_ref, w_pair_ref, x_keep, x_got, piece):
    many = sum(len(slots) for slots in slot_groups)
    count = x_keep.shape[0] // (many * piece)
    before = 0
    for n, slots in enumerate(slot_groups):
        each = len(slots) * piece
        for a in range(count):
            at = (a * many + before) * piece
            x_keep[at : at + each, :] = halves[2 * n][a * each : (a + 1) * each, :]
            x_got[at : at + each, :] = halves[2 * n + 1][a * each : (a + 1) * each, :]
        before += len(slots)
    return jnp.dot(x_keep[...], w_ref[...], preferred_element_type=jnp.float32) + jnp.dot(
        x_got[...], w_pair_ref[...], preferred_element_type=jnp.float32
    )


def project_early_kernel(piece, slot_groups, *refs):
    halves, (w_ref, w_pair_ref, out_ref, x_keep, x_got) = refs[:-5], refs[-5:]
    total = project_rows(slot_groups, halves, w_ref, w_pair_ref, x_keep, x_got, piece)
    out_ref[...] = total.astype(jnp.bfloat16)


def project_kernel(group, half, parts, early_groups, late_groups, *refs):
    halves, refs = refs[: 2 * len(late_groups)], refs[2 * len(late_groups) :]
    early_ref, w_ref, w_pair_ref, refs = refs[0], refs[1], refs[2], refs[3:]
    out_refs, (x_keep, x_got, late_ref) = refs[:-3], refs[-3:]
    count = len(out_refs)
    piece = out_refs[0].shape[0] // parts
    me = lax.axis_index("ctx")
    total = project_rows(late_groups, halves, w_ref, w_pair_ref, x_keep, x_got, piece)
    late_ref[...] = total.astype(jnp.bfloat16)
    mine = lax.rem(me, group) * half + lax.div(lax.axis_index("head"), 2)
    mine = jnp.bitwise_xor(mine, turn_of(lax.div(me, group), count))
    for k, out_ref in enumerate(out_refs):
        a = jnp.bitwise_xor(mine, k)
        for held, slot_groups in ((early_ref, early_groups), (late_ref, late_groups)):
            slots = [slot for some in slot_groups for slot in some]
            for i, slot in enumerate(slots):
                d = jnp.bitwise_xor(me, slot)
                at = pl.multiple_of((a * len(slots) + i) * piece, piece)
                out_ref[pl.ds(pl.multiple_of(d * piece, piece), piece), :] = held[pl.ds(at, piece), :]


def final_kernel(group, half, *refs):
    blocks, out_ref = refs[:-1], refs[-1]
    cols = blocks[0].shape[1]
    high = lax.div(lax.axis_index("ctx"), 2)
    high = jnp.bitwise_xor(high, turn_of(lax.axis_index("head"), len(blocks)))
    for first in range(0, len(blocks), half):
        part = lax.div(jnp.bitwise_xor(high, first), half)
        total = blocks[first][...].astype(jnp.float32)
        for k in range(first + 1, first + half):
            total = total + blocks[k][...].astype(jnp.float32)
        out_ref[:, pl.ds(pl.multiple_of(part * cols, cols), cols)] = total.astype(jnp.bfloat16)


def along_ctx(x, parts, k):
    return lax.ppermute(x, "ctx", [(i, i ^ k) for i in range(parts)])


def spread_first(block, q_block, kv_block, parts):
    half = parts // 2
    near, far_kv = {0: block}, {}
    far_kv[0] = along_ctx(kv_block, parts, half)
    far_kv[1] = along_ctx(kv_block, parts, half + 1)
    for k in [*range(2, half, 2), 1]:
        near[k] = along_ctx(block, parts, k)
    far_q = along_ctx(q_block, parts, half)
    near, far_kv = lax.optimization_barrier((near, far_kv))
    for k in range(2, half, 2):
        near[k + 1] = along_ctx(near[k], parts, 1)
        far_kv[k] = along_ctx(far_kv[0], parts, k)
        far_kv[k + 1] = along_ctx(far_kv[1], parts, k)
    return [near[k] for k in range(half)], [far_kv[k] for k in range(half)], far_q


def spread_second(far_q, parts):
    half = parts // 2
    got = {k: along_ctx(far_q, parts, k) for k in [*range(2, half, 2), 1]}
    return lax.optimization_barrier(got)


def spread_third(far_q, got, parts):
    half = parts // 2
    for k in range(2, half, 2):
        got[k + 1] = along_ctx(got[k], parts, 1)
    return [far_q] + [got[k] for k in range(1, half)]


def packed_body(groups, queries, keys, values, doc_ids, plan, w_out):
    parts = lax.axis_size("ctx")
    rows = queries.shape[0]
    heads = queries.shape[1] // HEAD_DIM
    width = w_out.shape[1]
    group, half = parts // groups, groups // 2
    bf16 = jnp.bfloat16
    params = pltpu.CompilerParams(vmem_limit_bytes=VMEM_LIMIT)
    pair = [(g, g ^ 1) for g in range(groups)]
    kv_rows = 2 * rows + META
    w_pair = lax.ppermute(w_out, "head", pair)
    block, q_block, kv_block = pl.pallas_call(
        functools.partial(pack_kernel, parts, heads),
        out_shape=[
            jax.ShapeDtypeStruct((heads * rows + kv_rows, HEAD_DIM), bf16),
            jax.ShapeDtypeStruct((heads * rows, HEAD_DIM), bf16),
            jax.ShapeDtypeStruct((kv_rows, HEAD_DIM), bf16),
        ],
        in_specs=[SMEM, VMEM, VMEM, VMEM, VMEM],
        out_specs=[VMEM] * 3,
        compiler_params=pltpu.CompilerParams(vmem_limit_bytes=PACK_LIMIT),
        name="pack",
    )(plan, queries, keys, values, doc_ids.reshape(1, rows))
    near, far_kv, far_q = spread_first(block, q_block, kv_block, parts)
    count = parts // 2
    arrived, halves = [], []
    last = parts - 1
    slot_groups = [range(half), range(half, count), range(count, count + 1), range(count + 1, last), range(last, parts)]
    for slots in slot_groups:
        inputs = [*near, *far_kv]
        if slots[0] >= count:
            inputs += far_q[slots[0] - count : slots[-1] + 1 - count]
        many = len(slots)
        out_rows = count * many * rows // parts
        send, keep = pl.pallas_call(
            functools.partial(attend_kernel, parts, heads, 1.0 / math.sqrt(HEAD_DIM), tuple(slots)),
            out_shape=[jax.ShapeDtypeStruct((out_rows, heads * HEAD_DIM), bf16)] * 2,
            in_specs=[VMEM] * len(inputs),
            out_specs=[VMEM, VMEM],
            scratch_shapes=[
                pltpu.VMEM((many, heads * rows, HEAD_DIM), bf16),
                pltpu.VMEM((parts, kv_rows, HEAD_DIM), bf16),
                pltpu.VMEM((2, out_rows, heads * HEAD_DIM), bf16),
                pltpu.SMEM((2, parts), jnp.float32),
            ],
            compiler_params=params,
            name="attend",
        )(*inputs)
        if slots[0] == 0:
            send, far_q = lax.optimization_barrier((send, far_q))
            second = spread_second(far_q, parts)
            far_q = [far_q]
        if slots[0] == count:
            send, halves[-2], second = lax.optimization_barrier((send, halves[-2], second))
            far_q = spread_third(far_q[0], second, parts)
        halves += [keep, lax.ppermute(send, "head", pair)]
    depth, piece = heads * HEAD_DIM, rows // parts
    early_groups, late_groups = slot_groups[:3], slot_groups[3:]
    early_rows, late_rows = [
        count * piece * sum(len(slots) for slots in some) for some in (early_groups, late_groups)
    ]
    early = pl.pallas_call(
        functools.partial(project_early_kernel, piece, early_groups),
        out_shape=jax.ShapeDtypeStruct((early_rows, width), bf16),
        in_specs=[VMEM] * (2 * len(early_groups) + 2),
        out_specs=VMEM,
        scratch_shapes=[pltpu.VMEM((early_rows, depth), bf16)] * 2,
        compiler_params=params,
        name="project_early",
    )(*halves[: 2 * len(early_groups)], w_out, w_pair)
    sums = pl.pallas_call(
        functools.partial(project_kernel, group, half, parts, early_groups, late_groups),
        out_shape=[jax.ShapeDtypeStruct((rows, width), bf16)] * count,
        in_specs=[VMEM] * (2 * len(late_groups) + 3),
        out_specs=[VMEM] * count,
        scratch_shapes=[
            pltpu.VMEM((late_rows, depth), bf16),
            pltpu.VMEM((late_rows, depth), bf16),
            pltpu.VMEM((late_rows, width), bf16),
        ],
        compiler_params=params,
        name="project",
    )(*halves[2 * len(early_groups) :], early, w_out, w_pair)
    for k in range(count):
        pairs = []
        for c in range(parts):
            for g in range(groups):
                high = ((c % group) * half + g // 2) ^ k ^ turn_of(c // group, count)
                pairs.append((c * groups + g, (high * 2 + g % 2) * groups + c // group))
        arrived.append(lax.ppermute(sums[k], ("ctx", "head"), pairs))
    return pl.pallas_call(
        functools.partial(final_kernel, group, half),
        out_shape=jax.ShapeDtypeStruct((rows, group * width), bf16),
        in_specs=[VMEM] * count,
        out_specs=VMEM,
        compiler_params=params,
        name="final_sum",
    )(*arrived)


def spread_rows(block, order, parts):
    shaped = block.reshape(parts, block.shape[0] // parts, block.shape[1])
    return jnp.take(shaped, order, axis=0).reshape(block.shape)


def attend(query_rows, row_pos, row_start, all_keys, all_values):
    n_rows = query_rows.shape[0]
    kv_local = all_keys.shape[1] // HEAD_DIM
    group_size = query_rows.shape[1] // all_keys.shape[1]
    q_heads = query_rows.reshape(n_rows, kv_local, group_size, HEAD_DIM).transpose(1, 0, 2, 3)
    q_heads = q_heads.reshape(kv_local, n_rows * group_size, HEAD_DIM)
    pos_rows = jnp.repeat(row_pos, group_size)
    start_rows = jnp.repeat(row_start, group_size)
    q_block = min(n_rows, max(1, 512 // group_size))
    block_rows = q_block * group_size
    n_qblocks = n_rows // q_block
    score_scale = 1.0 / math.sqrt(HEAD_DIM)
    total_keys = all_keys.shape[0]
    key_size = math.gcd(total_keys, 512)
    n_kblocks = total_keys // key_size
    key_tiles = all_keys.reshape(n_kblocks, key_size, kv_local, HEAD_DIM)
    value_tiles = all_values.reshape(n_kblocks, key_size, kv_local, HEAD_DIM)
    initial = (
        jnp.full((kv_local, n_rows * group_size), NEG_FILL, jnp.float32),
        jnp.zeros((kv_local, n_rows * group_size), jnp.float32),
        jnp.zeros((kv_local, n_rows * group_size, HEAD_DIM), jnp.float32),
    )

    def one_query_block(block_index, state):
        run_max, run_sum, run_acc = state
        offset = block_index * block_rows
        q_part = lax.dynamic_slice_in_dim(q_heads, offset, block_rows, 1)
        pos_part = lax.dynamic_slice_in_dim(pos_rows, offset, block_rows, 0)
        start_part = lax.dynamic_slice_in_dim(start_rows, offset, block_rows, 0)
        first_block = jnp.clip(jnp.min(start_part) // key_size, 0, n_kblocks)
        last_block = jnp.clip(jnp.max(pos_part) // key_size + 1, 0, n_kblocks)

        def add_tile(key_index, inner):
            block_max, block_sum, block_acc = inner
            key_tile = lax.dynamic_index_in_dim(key_tiles, key_index, 0, keepdims=False)
            value_tile = lax.dynamic_index_in_dim(value_tiles, key_index, 0, keepdims=False)
            scores = (
                jnp.einsum("grd,kgd->grk", q_part, key_tile, preferred_element_type=jnp.float32)
                * score_scale
            )
            key_pos = key_index * key_size + jnp.arange(key_size, dtype=jnp.int32)
            allowed = (key_pos[None, :] >= start_part[:, None]) & (
                key_pos[None, :] <= pos_part[:, None]
            )
            scores = jnp.where(allowed[None], scores, NEG_FILL)
            new_max = jnp.maximum(block_max, jnp.max(scores, axis=-1))
            expo = jnp.where(allowed[None], jnp.exp(scores - new_max[..., None]), 0.0)
            rescale = jnp.exp(block_max - new_max)
            block_sum = block_sum * rescale + jnp.sum(expo, axis=-1)
            block_acc = block_acc * rescale[..., None] + jnp.einsum(
                "grk,kgd->grd",
                expo.astype(jnp.bfloat16),
                value_tile,
                preferred_element_type=jnp.float32,
            )
            return (new_max, block_sum, block_acc)

        def one_key_block(key_index, inner):
            tile_low = key_index * key_size
            tile_high = tile_low + key_size - 1
            meets = jnp.any((start_part <= tile_high) & (pos_part >= tile_low))
            return lax.cond(
                meets, lambda carried: add_tile(key_index, carried), lambda carried: carried, inner
            )

        inner = (
            lax.dynamic_slice_in_dim(run_max, offset, block_rows, 1),
            lax.dynamic_slice_in_dim(run_sum, offset, block_rows, 1),
            lax.dynamic_slice_in_dim(run_acc, offset, block_rows, 1),
        )
        new_max, new_sum, new_acc = lax.fori_loop(first_block, last_block, one_key_block, inner)
        run_max = lax.dynamic_update_slice_in_dim(run_max, new_max, offset, 1)
        run_sum = lax.dynamic_update_slice_in_dim(run_sum, new_sum, offset, 1)
        run_acc = lax.dynamic_update_slice_in_dim(run_acc, new_acc, offset, 1)
        return (run_max, run_sum, run_acc)

    final_max, final_sum, final_acc = lax.fori_loop(0, n_qblocks, one_query_block, initial)
    result = final_acc / final_sum[..., None]
    result = result.reshape(kv_local, n_rows, group_size, HEAD_DIM).transpose(1, 0, 2, 3)
    return result.reshape(n_rows, kv_local * group_size * HEAD_DIM).astype(jnp.bfloat16)


def body(queries, keys, values, doc_ids, plan, w_out):
    n_rows = queries.shape[0]
    parts = lax.axis_size("ctx")
    my_index = lax.axis_index("ctx")
    all_ids, all_plan = (
        lax.all_gather(doc_ids, "ctx", axis=0, tiled=True),
        lax.all_gather(plan, "ctx", axis=0, tiled=True),
    )
    all_keys, all_values = (
        lax.all_gather(keys, "ctx", axis=0, tiled=True),
        lax.all_gather(values, "ctx", axis=0, tiled=True),
    )
    doc_range = jnp.arange(DOCS, dtype=jnp.int32)
    doc_first = jnp.sum((all_ids[None, :] < doc_range[:, None]).astype(jnp.int32), axis=1)
    local_pos = my_index * n_rows + jnp.arange(n_rows, dtype=jnp.int32)
    ids_here = jnp.take(all_ids, local_pos)
    local_out = attend(
        queries,
        local_pos,
        jnp.sum(jnp.where(ids_here[:, None] == doc_range[None, :], doc_first[None, :], 0), axis=1),
        all_keys,
        all_values,
    )
    attended = lax.all_to_all(
        spread_rows(local_out, plan[0], parts), "ctx", split_axis=0, concat_axis=0, tiled=True
    )
    stacked = jnp.dot(
        lax.all_gather(attended, "ctx", axis=0, tiled=True),
        w_out,
        preferred_element_type=jnp.float32,
    )
    partial_sum = lax.all_to_all(
        stacked.astype(jnp.bfloat16), "ctx", split_axis=0, concat_axis=1, tiled=True
    ).astype(stacked.dtype)
    summed = lax.psum_scatter(
        partial_sum.astype(jnp.bfloat16), "head", scatter_dimension=1, tiled=True
    )
    return summed


def fits(parts, groups, rows, width):
    powers = all(n & (n - 1) == 0 for n in (parts, groups))
    window = parts * rows * width * 2
    whole = rows % (16 * parts) == 0 and groups % 2 == 0 and parts % groups == 0
    return powers and whole and 8 * window <= VMEM_LIMIT


def solution(mesh):
    parts, groups = mesh.shape["ctx"], mesh.shape["head"]

    def one_device(queries, keys, values, doc_ids, plan, w_out):
        one_pair = keys.shape[1] == HEAD_DIM
        if one_pair and fits(parts, groups, queries.shape[0], queries.shape[1]):
            return packed_body(groups, queries, keys, values, doc_ids, plan, w_out)
        return body(queries, keys, values, doc_ids, plan, w_out)

    return jax.shard_map(
        one_device,
        mesh=mesh,
        in_specs=(
            P("ctx", "head"),
            P("ctx", "head"),
            P("ctx", "head"),
            P("ctx"),
            P("ctx", None),
            P("head", "ctx"),
        ),
        out_specs=P("ctx", "head"),
        check_vma=False,
    )
```

```python
import functools
import math

import jax
import jax.numpy as jnp
from jax import lax
from jax.experimental import pallas as pl
from jax.experimental.pallas import tpu as pltpu
from jax.sharding import PartitionSpec as P

HEAD_DIM = 128
DOCS = 16
META = 16
NEG_FILL = -1e30
VMEM_LIMIT = 24 * 1024 * 1024
PACK_LIMIT = 56 * 1024 * 1024

ANY = pl.BlockSpec(memory_space=pl.ANY)
VMEM = pl.BlockSpec(memory_space=pltpu.VMEM)


def pack_kernel(
    parts, heads, plan_ref, q_ref, k_ref, v_ref, ids_ref, all_out, q_out, kv_out,
    plan_held, q_held, held, ids_held, sems,
):
    rows = q_ref.shape[0]
    piece = rows // parts
    base = heads * rows
    pairs = [
        (plan_ref, plan_held),
        (ids_ref, ids_held),
        (k_ref, held.at[base : base + rows]),
        (v_ref, held.at[base + rows : base + 2 * rows]),
        (q_ref, q_held),
        (held.at[base:], kv_out),
        (held, all_out),
        (held.at[:base], q_out),
    ]
    copies = [pltpu.make_async_copy(*pair, sems.at[n]) for n, pair in enumerate(pairs)]
    for copy in copies[:5]:
        copy.start()
    copies[0].wait()
    lane = lax.broadcasted_iota(jnp.int32, (1, rows), 1)
    source = jnp.zeros((1, rows), jnp.int32)
    for j in range(parts):
        inside = (lane >= j * piece) & (lane < (j + 1) * piece)
        source = jnp.where(inside, (plan_held[0, j] - j) * piece + lane, source)
    row = lax.broadcasted_iota(jnp.int32, (META, rows), 0)
    from_row = lax.broadcasted_iota(jnp.int32, (rows, rows), 0)
    chosen = (from_row == source).astype(jnp.float32)
    positions = jnp.broadcast_to(source.astype(jnp.float32), (META, rows))
    copies[1].wait()
    ids_rows = jnp.broadcast_to(ids_held[...].astype(jnp.float32), (META, rows))
    ids_moved = jnp.dot(ids_rows, chosen, preferred_element_type=jnp.float32)
    meta = jnp.where(row == 0, ids_rows, jnp.where(row == 1, ids_moved, positions))
    held[base + 2 * rows :, :] = meta.astype(jnp.bfloat16)
    copies[2].wait()
    copies[3].wait()
    copies[5].start()
    copies[4].wait()
    for j in range(parts):
        p = plan_held[0, j]
        for h in range(heads):
            held[h * rows + j * piece : h * rows + (j + 1) * piece, :] = q_held[
                pl.ds(pl.multiple_of(p * piece, piece), piece), h * HEAD_DIM : (h + 1) * HEAD_DIM
            ]
    copies[6].start()
    copies[7].start()
    for copy in copies[5:]:
        copy.wait()


def attend_kernel(parts, heads, scale, slots, *refs):
    half, many = parts // 2, len(slots)
    near, far, refs = refs[:half], refs[half : 2 * half], refs[2 * half :]
    q_blocks = [near[k] for k in slots if k < half]
    if not q_blocks:
        q_blocks, refs = refs[:many], refs[many:]
    send_ref, keep_ref, q_held, kv_held, rows_ref, ends = refs
    rows = q_held.shape[1] // heads
    piece = rows // parts
    me = lax.axis_index("ctx")
    other = 1 - lax.rem(lax.axis_index("head"), 2)
    q_rows = heads * rows
    for k in range(half):
        kv_held[jnp.bitwise_xor(me, k)] = near[k][q_rows:, :]
        kv_held[jnp.bitwise_xor(me, half + k)] = far[k][...]
    for i in range(many):
        q_held[i] = q_blocks[i][:q_rows, :]

    def ids_of(block):
        return kv_held[block, 2 * rows :, :].astype(jnp.float32)

    for b in range(parts):
        ids = ids_of(b)[0:1]
        ends[0, b] = jnp.min(ids)
        ends[1, b] = jnp.max(ids)

    def one_block(i, carry):
        d = jnp.bitwise_xor(me, slots[0] + i)
        turned = ids_of(d).T
        q_ids, q_pos = turned[:, 1:2], turned[:, 2:3]
        start = jnp.int32(0)
        for b in range(parts):
            start = start + (ends[1, b] < ends[0, d]).astype(jnp.int32)
        b0 = lax.div(start, 2) * 2
        tiles = lax.div(d, 2) + 1 - lax.div(start, 2)
        for w in range(1, half + 1):

            @pl.when(tiles == w)
            def _(w=w):
                span = 2 * w * rows
                k_ids = jnp.concatenate([ids_of(b0 + n)[0:1] for n in range(2 * w)], axis=1)
                k_pos = lax.broadcasted_iota(jnp.int32, (1, span), 1) + (b0 - d) * rows
                allowed = (k_ids == q_ids) & (k_pos.astype(jnp.float32) <= q_pos)
                bias = jnp.where(allowed, 0.0, NEG_FILL)
                keys = kv_held[pl.ds(b0, 2 * w), :rows, :].reshape(span, HEAD_DIM)
                vals = kv_held[pl.ds(b0, 2 * w), rows : 2 * rows, :].reshape(span, HEAD_DIM)
                vals = jnp.concatenate([vals, jnp.ones((span, HEAD_DIM), jnp.bfloat16)], axis=1)
                for h in range(heads):
                    q = q_held[i, h * rows : (h + 1) * rows, :]
                    s = lax.dot_general(
                        q, keys, (((1,), (1,)), ((), ())), preferred_element_type=jnp.float32
                    )
                    s = s + bias
                    top = jnp.max(s, axis=1, keepdims=True)
                    e = jnp.exp2((s - top) * (scale * math.log2(math.e)))
                    o = jnp.dot(e.astype(jnp.bfloat16), vals, preferred_element_type=jnp.float32)
                    o = (o[:, :HEAD_DIM] / o[:, HEAD_DIM:]).astype(jnp.bfloat16)
                    for j in range(parts):
                        at = pl.multiple_of((j // 2) * many * piece + i * piece, piece)
                        rows_ref[
                            jnp.bitwise_xor(other, j % 2),
                            pl.ds(at, piece),
                            h * HEAD_DIM : (h + 1) * HEAD_DIM,
                        ] = o[j * piece : (j + 1) * piece, :]

        return carry

    lax.fori_loop(0, many, one_block, 0)
    send_ref[...] = rows_ref[0]
    keep_ref[...] = rows_ref[1]


def turn_of(plane, count):
    return (1 - (plane ^ (plane >> 1)) % 2) * (count - 1)


def project_rows(slot_groups, halves, w_ref, w_pair_ref, x_keep, x_got, piece):
    many = sum(len(slots) for slots in slot_groups)
    count = x_keep.shape[0] // (many * piece)
    before = 0
    for n, slots in enumerate(slot_groups):
        each = len(slots) * piece
        for a in range(count):
            at = (a * many + before) * piece
            x_keep[at : at + each, :] = halves[2 * n][a * each : (a + 1) * each, :]
            x_got[at : at + each, :] = halves[2 * n + 1][a * each : (a + 1) * each, :]
        before += len(slots)
    return jnp.dot(x_keep[...], w_ref[...], preferred_element_type=jnp.float32) + jnp.dot(
        x_got[...], w_pair_ref[...], preferred_element_type=jnp.float32
    )


def project_early_kernel(piece, slot_groups, *refs):
    halves, (w_ref, w_pair_ref, out_ref, x_keep, x_got) = refs[:-5], refs[-5:]
    total = project_rows(slot_groups, halves, w_ref, w_pair_ref, x_keep, x_got, piece)
    out_ref[...] = total.astype(jnp.bfloat16)


def project_kernel(group, half, parts, early_groups, late_groups, *refs):
    halves, refs = refs[: 2 * len(late_groups)], refs[2 * len(late_groups) :]
    early_ref, w_ref, w_pair_ref, refs = refs[0], refs[1], refs[2], refs[3:]
    out_refs, (x_keep, x_got, late_ref) = refs[:-3], refs[-3:]
    count = len(out_refs)
    piece = out_refs[0].shape[0] // parts
    me = lax.axis_index("ctx")
    total = project_rows(late_groups, halves, w_ref, w_pair_ref, x_keep, x_got, piece)
    late_ref[...] = total.astype(jnp.bfloat16)
    mine = lax.rem(me, group) * half + lax.div(lax.axis_index("head"), 2)
    mine = jnp.bitwise_xor(mine, turn_of(lax.div(me, group), count))
    for k, out_ref in enumerate(out_refs):
        a = jnp.bitwise_xor(mine, k)
        for held, slot_groups in ((early_ref, early_groups), (late_ref, late_groups)):
            slots = [slot for some in slot_groups for slot in some]
            for i, slot in enumerate(slots):
                d = jnp.bitwise_xor(me, slot)
                at = pl.multiple_of((a * len(slots) + i) * piece, piece)
                out_ref[pl.ds(pl.multiple_of(d * piece, piece), piece), :] = held[pl.ds(at, piece), :]


def final_kernel(group, half, *refs):
    blocks, out_ref = refs[:-1], refs[-1]
    cols = blocks[0].shape[1]
    high = lax.div(lax.axis_index("ctx"), 2)
    high = jnp.bitwise_xor(high, turn_of(lax.axis_index("head"), len(blocks)))
    for first in range(0, len(blocks), half):
        part = lax.div(jnp.bitwise_xor(high, first), half)
        total = blocks[first][...].astype(jnp.float32)
        for k in range(first + 1, first + half):
            total = total + blocks[k][...].astype(jnp.float32)
        out_ref[:, pl.ds(pl.multiple_of(part * cols, cols), cols)] = total.astype(jnp.bfloat16)


def along_ctx(x, parts, k):
    return lax.ppermute(x, "ctx", [(i, i ^ k) for i in range(parts)])


def spread_first(block, q_block, kv_block, parts):
    half = parts // 2
    near, far_kv = {0: block}, {}
    far_kv[0] = along_ctx(kv_block, parts, half)
    far_kv[1] = along_ctx(kv_block, parts, half + 1)
    for k in [*range(2, half, 2), 1]:
        near[k] = along_ctx(block, parts, k)
    far_q = along_ctx(q_block, parts, half)
    near, far_kv = lax.optimization_barrier((near, far_kv))
    for k in range(2, half, 2):
        near[k + 1] = along_ctx(near[k], parts, 1)
        far_kv[k] = along_ctx(far_kv[0], parts, k)
        far_kv[k + 1] = along_ctx(far_kv[1], parts, k)
    return [near[k] for k in range(half)], [far_kv[k] for k in range(half)], far_q


def spread_second(far_q, parts):
    half = parts // 2
    got = {k: along_ctx(far_q, parts, k) for k in [*range(2, half, 2), 1]}
    return lax.optimization_barrier(got)


def spread_third(far_q, got, parts):
    half = parts // 2
    for k in range(2, half, 2):
        got[k + 1] = along_ctx(got[k], parts, 1)
    return [far_q] + [got[k] for k in range(1, half)]


def packed_body(groups, queries, keys, values, doc_ids, plan, w_out):
    parts = lax.axis_size("ctx")
    rows = queries.shape[0]
    heads = queries.shape[1] // HEAD_DIM
    width = w_out.shape[1]
    group, half = parts // groups, groups // 2
    bf16 = jnp.bfloat16
    params = pltpu.CompilerParams(vmem_limit_bytes=VMEM_LIMIT)
    pair = [(g, g ^ 1) for g in range(groups)]
    kv_rows = 2 * rows + META
    w_pair = lax.ppermute(w_out, "head", pair)
    block, q_block, kv_block = pl.pallas_call(
        functools.partial(pack_kernel, parts, heads),
        out_shape=[
            jax.ShapeDtypeStruct((heads * rows + kv_rows, HEAD_DIM), bf16),
            jax.ShapeDtypeStruct((heads * rows, HEAD_DIM), bf16),
            jax.ShapeDtypeStruct((kv_rows, HEAD_DIM), bf16),
        ],
        in_specs=[ANY] * 5,
        out_specs=[ANY] * 3,
        scratch_shapes=[
            pltpu.SMEM(plan.shape, jnp.int32),
            pltpu.VMEM(queries.shape, bf16),
            pltpu.VMEM((heads * rows + kv_rows, HEAD_DIM), bf16),
            pltpu.VMEM((1, rows), jnp.int32),
            pltpu.SemaphoreType.DMA((8,)),
        ],
        compiler_params=pltpu.CompilerParams(vmem_limit_bytes=PACK_LIMIT),
        name="pack",
    )(plan, queries, keys, values, doc_ids.reshape(1, rows))
    near, far_kv, far_q = spread_first(block, q_block, kv_block, parts)
    count = parts // 2
    arrived, halves = [], []
    last = parts - 1
    slot_groups = [range(half), range(half, count), range(count, count + 1), range(count + 1, last), range(last, parts)]
    for slots in slot_groups:
        inputs = [*near, *far_kv]
        if slots[0] >= count:
            inputs += far_q[slots[0] - count : slots[-1] + 1 - count]
        many = len(slots)
        out_rows = count * many * rows // parts
        send, keep = pl.pallas_call(
            functools.partial(attend_kernel, parts, heads, 1.0 / math.sqrt(HEAD_DIM), tuple(slots)),
            out_shape=[jax.ShapeDtypeStruct((out_rows, heads * HEAD_DIM), bf16)] * 2,
            in_specs=[VMEM] * len(inputs),
            out_specs=[VMEM, VMEM],
            scratch_shapes=[
                pltpu.VMEM((many, heads * rows, HEAD_DIM), bf16),
                pltpu.VMEM((parts, kv_rows, HEAD_DIM), bf16),
                pltpu.VMEM((2, out_rows, heads * HEAD_DIM), bf16),
                pltpu.SMEM((2, parts), jnp.float32),
            ],
            compiler_params=params,
            name="attend",
        )(*inputs)
        if slots[0] == 0:
            send, far_q = lax.optimization_barrier((send, far_q))
            second = spread_second(far_q, parts)
            far_q = [far_q]
        if slots[0] == count:
            send, halves[-2], second = lax.optimization_barrier((send, halves[-2], second))
            far_q = spread_third(far_q[0], second, parts)
        halves += [keep, lax.ppermute(send, "head", pair)]
    depth, piece = heads * HEAD_DIM, rows // parts
    early_groups, late_groups = slot_groups[:3], slot_groups[3:]
    early_rows, late_rows = [
        count * piece * sum(len(slots) for slots in some) for some in (early_groups, late_groups)
    ]
    early = pl.pallas_call(
        functools.partial(project_early_kernel, piece, early_groups),
        out_shape=jax.ShapeDtypeStruct((early_rows, width), bf16),
        in_specs=[VMEM] * (2 * len(early_groups) + 2),
        out_specs=VMEM,
        scratch_shapes=[pltpu.VMEM((early_rows, depth), bf16)] * 2,
        compiler_params=params,
        name="project_early",
    )(*halves[: 2 * len(early_groups)], w_out, w_pair)
    sums = pl.pallas_call(
        functools.partial(project_kernel, group, half, parts, early_groups, late_groups),
        out_shape=[jax.ShapeDtypeStruct((rows, width), bf16)] * count,
        in_specs=[VMEM] * (2 * len(late_groups) + 3),
        out_specs=[VMEM] * count,
        scratch_shapes=[
            pltpu.VMEM((late_rows, depth), bf16),
            pltpu.VMEM((late_rows, depth), bf16),
            pltpu.VMEM((late_rows, width), bf16),
        ],
        compiler_params=params,
        name="project",
    )(*halves[2 * len(early_groups) :], early, w_out, w_pair)
    for k in range(count):
        pairs = []
        for c in range(parts):
            for g in range(groups):
                high = ((c % group) * half + g // 2) ^ k ^ turn_of(c // group, count)
                pairs.append((c * groups + g, (high * 2 + g % 2) * groups + c // group))
        arrived.append(lax.ppermute(sums[k], ("ctx", "head"), pairs))
    return pl.pallas_call(
        functools.partial(final_kernel, group, half),
        out_shape=jax.ShapeDtypeStruct((rows, group * width), bf16),
        in_specs=[VMEM] * count,
        out_specs=VMEM,
        compiler_params=params,
        name="final_sum",
    )(*arrived)


def spread_rows(block, order, parts):
    shaped = block.reshape(parts, block.shape[0] // parts, block.shape[1])
    return jnp.take(shaped, order, axis=0).reshape(block.shape)


def attend(query_rows, row_pos, row_start, all_keys, all_values):
    n_rows = query_rows.shape[0]
    kv_local = all_keys.shape[1] // HEAD_DIM
    group_size = query_rows.shape[1] // all_keys.shape[1]
    q_heads = query_rows.reshape(n_rows, kv_local, group_size, HEAD_DIM).transpose(1, 0, 2, 3)
    q_heads = q_heads.reshape(kv_local, n_rows * group_size, HEAD_DIM)
    pos_rows = jnp.repeat(row_pos, group_size)
    start_rows = jnp.repeat(row_start, group_size)
    q_block = min(n_rows, max(1, 512 // group_size))
    block_rows = q_block * group_size
    n_qblocks = n_rows // q_block
    score_scale = 1.0 / math.sqrt(HEAD_DIM)
    total_keys = all_keys.shape[0]
    key_size = math.gcd(total_keys, 512)
    n_kblocks = total_keys // key_size
    key_tiles = all_keys.reshape(n_kblocks, key_size, kv_local, HEAD_DIM)
    value_tiles = all_values.reshape(n_kblocks, key_size, kv_local, HEAD_DIM)
    initial = (
        jnp.full((kv_local, n_rows * group_size), NEG_FILL, jnp.float32),
        jnp.zeros((kv_local, n_rows * group_size), jnp.float32),
        jnp.zeros((kv_local, n_rows * group_size, HEAD_DIM), jnp.float32),
    )

    def one_query_block(block_index, state):
        run_max, run_sum, run_acc = state
        offset = block_index * block_rows
        q_part = lax.dynamic_slice_in_dim(q_heads, offset, block_rows, 1)
        pos_part = lax.dynamic_slice_in_dim(pos_rows, offset, block_rows, 0)
        start_part = lax.dynamic_slice_in_dim(start_rows, offset, block_rows, 0)
        first_block = jnp.clip(jnp.min(start_part) // key_size, 0, n_kblocks)
        last_block = jnp.clip(jnp.max(pos_part) // key_size + 1, 0, n_kblocks)

        def add_tile(key_index, inner):
            block_max, block_sum, block_acc = inner
            key_tile = lax.dynamic_index_in_dim(key_tiles, key_index, 0, keepdims=False)
            value_tile = lax.dynamic_index_in_dim(value_tiles, key_index, 0, keepdims=False)
            scores = (
                jnp.einsum("grd,kgd->grk", q_part, key_tile, preferred_element_type=jnp.float32)
                * score_scale
            )
            key_pos = key_index * key_size + jnp.arange(key_size, dtype=jnp.int32)
            allowed = (key_pos[None, :] >= start_part[:, None]) & (
                key_pos[None, :] <= pos_part[:, None]
            )
            scores = jnp.where(allowed[None], scores, NEG_FILL)
            new_max = jnp.maximum(block_max, jnp.max(scores, axis=-1))
            expo = jnp.where(allowed[None], jnp.exp(scores - new_max[..., None]), 0.0)
            rescale = jnp.exp(block_max - new_max)
            block_sum = block_sum * rescale + jnp.sum(expo, axis=-1)
            block_acc = block_acc * rescale[..., None] + jnp.einsum(
                "grk,kgd->grd",
                expo.astype(jnp.bfloat16),
                value_tile,
                preferred_element_type=jnp.float32,
            )
            return (new_max, block_sum, block_acc)

        def one_key_block(key_index, inner):
            tile_low = key_index * key_size
            tile_high = tile_low + key_size - 1
            meets = jnp.any((start_part <= tile_high) & (pos_part >= tile_low))
            return lax.cond(
                meets, lambda carried: add_tile(key_index, carried), lambda carried: carried, inner
            )

        inner = (
            lax.dynamic_slice_in_dim(run_max, offset, block_rows, 1),
            lax.dynamic_slice_in_dim(run_sum, offset, block_rows, 1),
            lax.dynamic_slice_in_dim(run_acc, offset, block_rows, 1),
        )
        new_max, new_sum, new_acc = lax.fori_loop(first_block, last_block, one_key_block, inner)
        run_max = lax.dynamic_update_slice_in_dim(run_max, new_max, offset, 1)
        run_sum = lax.dynamic_update_slice_in_dim(run_sum, new_sum, offset, 1)
        run_acc = lax.dynamic_update_slice_in_dim(run_acc, new_acc, offset, 1)
        return (run_max, run_sum, run_acc)

    final_max, final_sum, final_acc = lax.fori_loop(0, n_qblocks, one_query_block, initial)
    result = final_acc / final_sum[..., None]
    result = result.reshape(kv_local, n_rows, group_size, HEAD_DIM).transpose(1, 0, 2, 3)
    return result.reshape(n_rows, kv_local * group_size * HEAD_DIM).astype(jnp.bfloat16)


def body(queries, keys, values, doc_ids, plan, w_out):
    n_rows = queries.shape[0]
    parts = lax.axis_size("ctx")
    my_index = lax.axis_index("ctx")
    all_ids, all_plan = (
        lax.all_gather(doc_ids, "ctx", axis=0, tiled=True),
        lax.all_gather(plan, "ctx", axis=0, tiled=True),
    )
    all_keys, all_values = (
        lax.all_gather(keys, "ctx", axis=0, tiled=True),
        lax.all_gather(values, "ctx", axis=0, tiled=True),
    )
    doc_range = jnp.arange(DOCS, dtype=jnp.int32)
    doc_first = jnp.sum((all_ids[None, :] < doc_range[:, None]).astype(jnp.int32), axis=1)
    local_pos = my_index * n_rows + jnp.arange(n_rows, dtype=jnp.int32)
    ids_here = jnp.take(all_ids, local_pos)
    local_out = attend(
        queries,
        local_pos,
        jnp.sum(jnp.where(ids_here[:, None] == doc_range[None, :], doc_first[None, :], 0), axis=1),
        all_keys,
        all_values,
    )
    attended = lax.all_to_all(
        spread_rows(local_out, plan[0], parts), "ctx", split_axis=0, concat_axis=0, tiled=True
    )
    stacked = jnp.dot(
        lax.all_gather(attended, "ctx", axis=0, tiled=True),
        w_out,
        preferred_element_type=jnp.float32,
    )
    partial_sum = lax.all_to_all(
        stacked.astype(jnp.bfloat16), "ctx", split_axis=0, concat_axis=1, tiled=True
    ).astype(stacked.dtype)
    summed = lax.psum_scatter(
        partial_sum.astype(jnp.bfloat16), "head", scatter_dimension=1, tiled=True
    )
    return summed


def fits(parts, groups, rows, width):
    powers = all(n & (n - 1) == 0 for n in (parts, groups))
    window = parts * rows * width * 2
    whole = rows % (16 * parts) == 0 and groups % 2 == 0 and parts % groups == 0
    return powers and whole and 8 * window <= VMEM_LIMIT


def solution(mesh):
    parts, groups = mesh.shape["ctx"], mesh.shape["head"]

    def one_device(queries, keys, values, doc_ids, plan, w_out):
        one_pair = keys.shape[1] == HEAD_DIM
        if one_pair and fits(parts, groups, queries.shape[0], queries.shape[1]):
            return packed_body(groups, queries, keys, values, doc_ids, plan, w_out)
        return body(queries, keys, values, doc_ids, plan, w_out)

    return jax.shard_map(
        one_device,
        mesh=mesh,
        in_specs=(
            P("ctx", "head"),
            P("ctx", "head"),
            P("ctx", "head"),
            P("ctx"),
            P("ctx", None),
            P("head", "ctx"),
        ),
        out_specs=P("ctx", "head"),
        check_vma=False,
    )
```
